256 devices in a mesh: depth: 16 (over z, x_lo), row: 4 (over y), col: 4 (over x_hi, core).
Axes of the slice: x: 4 (x_hi: 2, x_lo: 2; x = x_hi * 2 + x_lo), y: 4, z: 8, core: 2. Of those that a mesh axis runs over, the one named last changes fastest.
Arguments:
- layer_input: bfloat16 [8192, 4096], P(('depth', 'col'), 'row'), may hold values from -6 to 6
- out_grad: bfloat16 [8192, 4096], P(('depth', 'col'), 'row'), may hold values from -6 to 6
- gate_pre: bfloat16 [8192, 14336], P(('depth', 'row'), 'col'), may hold values from -6 to 6
- up_pre: bfloat16 [8192, 14336], P(('depth', 'row'), 'col'), may hold values from -6 to 6
- gate_weight: bfloat16 [4096, 14336], P('row', 'col'), may hold values from -0.09375 to 0.09375
- up_weight: bfloat16 [4096, 14336], P('row', 'col'), may hold values from -0.09375 to 0.09375
- down_weight: bfloat16 [14336, 4096], P('col', 'row'), may hold values from -0.046875 to 0.046875
- gate_first: bfloat16 [4096, 14336], P(('row', 'depth'), 'col'), may hold values from -18 to 18
- gate_second: bfloat16 [4096, 14336], P(('row', 'depth'), 'col'), may hold values from 1 to 100
- up_first: bfloat16 [4096, 14336], P(('row', 'depth'), 'col'), may hold values from -18 to 18
- up_second: bfloat16 [4096, 14336], P(('row', 'depth'), 'col'), may hold values from 1 to 100
- down_first: bfloat16 [14336, 4096], P(('col', 'depth'), 'row'), may hold values from -18 to 18
- down_second: bfloat16 [14336, 4096], P(('col', 'depth'), 'row'), may hold values from 1 to 100
Outputs:
- input_grad: bfloat16 [8192, 4096], P(('depth', 'col'), 'row')
- new_gate: bfloat16 [4096, 14336], P(('row', 'depth'), 'col')
- new_gate_first: bfloat16 [4096, 14336], P(('row', 'depth'), 'col')
- new_gate_second: bfloat16 [4096, 14336], P(('row', 'depth'), 'col')
- new_up: bfloat16 [4096, 14336], P(('row', 'depth'), 'col')
- new_up_first: bfloat16 [4096, 14336], P(('row', 'depth'), 'col')
- new_up_second: bfloat16 [4096, 14336], P(('row', 'depth'), 'col')
- new_down: bfloat16 [14336, 4096], P(('col', 'depth'), 'row')
- new_down_first: bfloat16 [14336, 4096], P(('col', 'depth'), 'row')
- new_down_second: bfloat16 [14336, 4096], P(('col', 'depth'), 'row')
The draws below stay inside these ranges and needn't reach their ends.
All inputs are finite; a program needn't handle non-finite values.
Results may differ from the reference program's by a relative error of at most 0.0052.
Values may be sent and summed in bfloat16 or wider, within the bound.
A program may use at most 256 MiB of HBM per device.

```python
import math
import jax
import jax.numpy as jnp
from jax import lax

D = 4096
FF = 14336
TOKENS = 8192


def shard_levels(rng, extent, cuts, least, top_value):
    def one(axis_at, parts):
        heights = jax.random.uniform(jax.random.fold_in(jax.random.fold_in(rng, 6), axis_at), (parts,), jnp.float32, least / len(cuts), top_value / len(cuts))
        return jnp.repeat(jnp.exp(heights), extent[axis_at] // parts).reshape((-1,) + (1,) * (len(extent) - axis_at - 1))

    factor_of = one(*cuts[0])
    for cut in cuts[1:]:
        factor_of = factor_of * one(*cut)
    return factor_of


def centred(stream_key, extent, deviation, limit, cuts=(), kind=jnp.bfloat16):
    loudness = shard_levels(stream_key, extent, cuts, -0.22, 0.18) if cuts else 1.0
    entries = jax.random.normal(stream_key, extent, jnp.float32) * deviation * loudness
    return jnp.minimum(jnp.maximum(entries, -limit), limit).astype(kind)


def setup_inputs(seed: int = 0) -> dict:
    seeds = jax.random.split(jax.random.key(seed), 14)
    layer_input = centred(seeds[0], (TOKENS, D), 1.0, 6.0, ((0, 64), (1, 4)))
    out_grad = centred(seeds[1], (TOKENS, D), 1.0, 6.0, ((0, 64), (1, 4)))
    gate_pre = centred(seeds[2], (TOKENS, FF), 1.0, 6.0, ((0, 64), (1, 4)))
    up_pre = centred(seeds[3], (TOKENS, FF), 1.0, 6.0, ((0, 64), (1, 4)))
    gate_weight = centred(seeds[4], (D, FF), D ** -0.5, 0.09375, ((0, 4), (1, 4)))
    up_weight = centred(seeds[5], (D, FF), D ** -0.5, 0.09375, ((0, 4), (1, 4)))
    down_weight = centred(seeds[6], (FF, D), FF ** -0.5, 0.046875, ((0, 4), (1, 4)))
    gate_first = centred(seeds[7], (D, FF), 3.0, 18.0, ((0, 64), (1, 4)))
    gate_second = jnp.clip(jnp.exp(math.log(100.0) - 4.6051702 * jax.random.uniform(seeds[8], (D, FF), jnp.float32) ** shard_levels(seeds[8], (D, FF), ((0, 64), (1, 4)), -0.2, 0.2)), 1.0, 100.0).astype(jnp.bfloat16)
    up_first = centred(seeds[9], (D, FF), 3.0, 18.0, ((0, 64), (1, 4)))
    up_second = jnp.clip(jnp.exp(math.log(100.0) - 4.6051702 * jax.random.uniform(seeds[10], (D, FF), jnp.float32) ** shard_levels(seeds[10], (D, FF), ((0, 64), (1, 4)), -0.2, 0.2)), 1.0, 100.0).astype(jnp.bfloat16)
    down_first = centred(seeds[11], (FF, D), 3.0, 18.0, ((0, 64), (1, 4)))
    down_second = jnp.clip(jnp.exp(math.log(100.0) - 4.6051702 * jax.random.uniform(seeds[12], (FF, D), jnp.float32) ** shard_levels(seeds[12], (FF, D), ((0, 64), (1, 4)), -0.2, 0.2)), 1.0, 100.0).astype(jnp.bfloat16)
    return {"layer_input": layer_input, "out_grad": out_grad, "gate_pre": gate_pre, "up_pre": up_pre, "gate_weight": gate_weight, "up_weight": up_weight, "down_weight": down_weight, "gate_first": gate_first, "gate_second": gate_second, "up_first": up_first, "up_second": up_second, "down_first": down_first, "down_second": down_second}


lr_rate = 0.0003
beta_one = 0.9
beta_two = 0.95
decay_rate = 0.1
eps_value = 1e-08
correct_one = 1.0 - 0.9 ** 20
correct_two = 1.0 - 0.95 ** 20

def swiglu_back(gate_pre, up_pre, hidden_grad):
    gate_val = gate_pre.astype(jnp.float32)
    up_val = up_pre.astype(jnp.float32)
    sig = jax.nn.sigmoid(gate_val)
    active = gate_val * sig
    hidden = (active * up_val).astype(jnp.bfloat16)
    gate_grad = (hidden_grad * up_val * sig * (1.0 + gate_val * (1.0 - sig))).astype(jnp.bfloat16)
    up_grad = (hidden_grad * active).astype(jnp.bfloat16)
    return (hidden, gate_grad, up_grad)

def adamw(weight, first, second, grad):
    first_new = beta_one * first.astype(jnp.float32) + (1.0 - beta_one) * grad
    second_new = beta_two * second.astype(jnp.float32) + (1.0 - beta_two) * grad * grad
    wval = weight.astype(jnp.float32)
    step_val = first_new / correct_one / (jnp.sqrt(second_new / correct_two) + eps_value) + decay_rate * wval
    new_weight = (wval - lr_rate * step_val).astype(jnp.bfloat16)
    return (new_weight, first_new.astype(jnp.bfloat16), second_new.astype(jnp.bfloat16))

def contract(left, right, left_dim, right_dim):
    return lax.dot_general(left, right, (((left_dim,), (right_dim,)), ((), ())), preferred_element_type=jnp.float32)

def reference(layer_input, out_grad, gate_pre, up_pre, gate_weight, up_weight, down_weight, gate_first, gate_second, up_first, up_second, down_first, down_second):
    hidden_grad = contract(out_grad, down_weight, 1, 1)
    hidden, gate_grad, up_grad = swiglu_back(gate_pre, up_pre, hidden_grad)
    input_grad = (contract(gate_grad, gate_weight, 1, 1) + contract(up_grad, up_weight, 1, 1)).astype(jnp.bfloat16)
    grad_gate = contract(layer_input, gate_grad, 0, 0)
    grad_up = contract(layer_input, up_grad, 0, 0)
    grad_down = contract(hidden, out_grad, 0, 0)
    new_gate, gate_m, gate_v = adamw(gate_weight, gate_first, gate_second, grad_gate)
    new_up, up_m, up_v = adamw(up_weight, up_first, up_second, grad_up)
    new_down, down_m, down_v = adamw(down_weight, down_first, down_second, grad_down)
    return (input_grad, new_gate, gate_m, gate_v, new_up, up_m, up_v, new_down, down_m, down_v)
```

```python
import jax
import jax.numpy as jnp
from jax import lax
from jax.experimental import pallas as pl
from jax.experimental.pallas import tpu as pltpu
from jax.sharding import PartitionSpec as P

BF = jnp.bfloat16
F32 = jnp.float32
MESH = pl.DeviceIdType.MESH

lr_rate = 0.0003
beta_one = 0.9
beta_two = 0.95
decay_rate = 0.1
eps_value = 1e-08
correct_one = 1.0 - 0.9**20
correct_two = 1.0 - 0.95**20

NZ = 8
CB = 512
NB = 7
NQ = 2 * NB
ZR = 128
UR = 448
DK = 4
DC = 256


def adamw(weight, first, second, grad):
    first_new = beta_one * first.astype(F32) + (1.0 - beta_one) * grad
    second_new = beta_two * second.astype(F32) + (1.0 - beta_two) * grad * grad
    wval = weight.astype(F32)
    step_val = (
        first_new / correct_one / (jnp.sqrt(second_new / correct_two) + eps_value)
        + decay_rate * wval
    )
    return (
        (wval - lr_rate * step_val).astype(BF),
        first_new.astype(BF),
        second_new.astype(BF),
    )


def dot_nn(a, b):
    return lax.dot_general(a, b, (((1,), (0,)), ((), ())), preferred_element_type=F32)


def dot_nt(a, b):
    return lax.dot_general(a, b, (((1,), (1,)), ((), ())), preferred_element_type=F32)


def rows_of(index, size):
    return pl.ds(pl.multiple_of(index * size, size), size)


def kernel(
    x_ref, do_ref, gp_ref, up_ref, wg, wu, wd, gm, gv, um, uv, dm, dv,
    ig_out, ng, ngm, ngv, nu, num, nuv, nd, ndm, ndv,
    do_all, xt_all, ht_all, gu, wdb, wgb, a_s, a_own, a_r,
    s0, rl, rs, fin, acc, xs, xr, abuf,
    s0d, rld, rsd, find, accd, xsd, xrd, dab,
    igacc, igs, igr, igo,
    do_ss, do_rs, xt_ss, xt_rs, ht_ss, ht_rs, a_ss, a_rs, b_ss, b_rs,
    l_ss, l_rs, h_ss, h_rs, x_ss, x_rs,
    dl_ss, dl_rs, dh_ss, dh_rs, dx_ss, dx_rs,
    ig_ss, ig_rs, wd_sem, wg_sem, ab_sem, ob_sem, da_sem, igo_sem,
):
    d = lax.axis_index("depth")
    r = lax.axis_index("row")
    c = lax.axis_index("col")
    z = lax.div(d, 2)
    xl = lax.rem(d, 2)

    def zmod(v):
        return lax.rem(v + 16, NZ)

    def zdev(v):
        return (2 * zmod(v) + xl, r, c)

    xdev = (2 * z + 1 - xl, r, c)

    def ydev(k):
        return (d, lax.rem(r + k, 4), c)

    def cdev(k):
        return (d, r, lax.rem(c + k, 4))

    def rc(src, dst, ss, rsem, dev):
        return pltpu.make_async_remote_copy(
            src_ref=src, dst_ref=dst, send_sem=ss, recv_sem=rsem,
            device_id=dev, device_id_type=MESH,
        )

    def lc(src, dst, sem):
        return pltpu.make_async_copy(src, dst, sem)

    def wd_copy(j, par):
        return lc(wd.at[rows_of(j, CB), :], wdb.at[par], wd_sem.at[par])

    def wg_start(q, par):
        cols = rows_of(lax.div(q, 2), CB)

        @pl.when(par == 0)
        def _():
            lc(wg.at[:, cols], wgb.at[0], wg_sem.at[0]).start()

        @pl.when(par == 1)
        def _():
            lc(wu.at[:, cols], wgb.at[1], wg_sem.at[1]).start()

    for p in range(2):
        wd_copy(p, p).start()
    lc(wg.at[:, pl.ds(0, CB)], wgb.at[0], wg_sem.at[0]).start()
    lc(wu.at[:, pl.ds(0, CB)], wgb.at[1], wg_sem.at[1]).start()
    lc(wd.at[rows_of(d, 224), :], dab.at[0], da_sem.at[0]).start()
    lc(dm, dab.at[1], da_sem.at[1]).start()
    lc(dv, dab.at[2], da_sem.at[2]).start()

    barrier = pltpu.get_barrier_semaphore()
    partners = [zdev(z + 1), zdev(z - 1), xdev]
    partners += [ydev(k) for k in (1, 2, 3)] + [cdev(k) for k in (1, 2, 3)]
    for dev in partners:
        pl.semaphore_signal(barrier, inc=1, device_id=dev, device_id_type=MESH)
    pl.semaphore_wait(barrier, len(partners))

    own_c = rows_of(c, 128)
    own_r = rows_of(r, 128)

    def do_copy(k):
        return rc(do_ref, do_all.at[own_c, :], do_ss.at[k - 1], do_rs.at[k - 1], cdev(k))

    for k in (2, 1, 3):
        do_copy(k).start()
    do_all[own_c, :] = do_ref[...]

    @pl.loop(0, NB)
    def _(j):
        cols = rows_of(j, CB)
        g = gp_ref[:, cols].astype(F32)
        h = g * jax.nn.sigmoid(g) * up_ref[:, cols].astype(F32)
        ht_all[cols, own_r] = h.T.astype(BF)

    def ht_copy(i, k):
        away = (2 * lax.rem(i, 2) - 1) * (4 - lax.div(i + 1, 2))
        view = ht_all.at[rows_of(zmod(z + away), UR), own_r]
        return rc(view, view, ht_ss.at[i, k - 1], ht_rs.at[i, k - 1], ydev(k))

    @pl.loop(0, NZ)
    def _(i):
        for k in (2, 1, 3):
            ht_copy(i, k).start()

    xt_all[:, own_c] = x_ref[...].T

    def xt_copy(k):
        view = xt_all.at[:, own_c]
        return rc(view, view, xt_ss.at[k - 1], xt_rs.at[k - 1], cdev(k))

    for k in (2, 1, 3):
        xt_copy(k).start()

    def a_copy(j, par, k):
        return rc(a_s.at[par, k - 1], a_r.at[j, k - 1], a_ss.at[par, k - 1],
                  a_rs.at[j, k - 1], ydev(k))

    def stage_a(j):
        par = lax.rem(j, 2)
        wd_copy(j, par).wait()

        @pl.when(j >= 2)
        def _():
            for k in (2, 1, 3):
                a_copy(j, par, k).wait_send()

        def part(k):
            return dot_nt(do_all[rows_of(lax.rem(r + k, 4), 128), :], wdb[par])

        for k in (2, 1, 3):
            a_s[par, k - 1] = part(k).astype(BF)
            a_copy(j, par, k).start()
        a_own[par] = part(0)

        @pl.when(j + 2 < NB)
        def _():
            wd_copy(j + 2, par).start()

    def b_copy(q, k):
        view = gu.at[q, own_r, :]
        return rc(view, view, b_ss.at[q, k - 1], b_rs.at[q, k - 1], ydev(k))

    def stage_b(j):
        par = lax.rem(j, 2)
        for k in (2, 1, 3):
            a_copy(j, par, k).wait_recv()

        @pl.loop(0, 8)
        def _(i):
            sub = rows_of(i, 16)
            cols = rows_of(j, CB)
            hg = a_own[par, sub, :]
            for k in range(3):
                hg += a_r[j, k, sub, :].astype(F32)
            g = gp_ref[sub, cols].astype(F32)
            u = up_ref[sub, cols].astype(F32)
            sig = jax.nn.sigmoid(g)
            dst = pl.ds(pl.multiple_of(r * 128 + i * 16, 16), 16)
            gu[2 * j, dst, :] = (hg * u * sig * (1.0 + g * (1.0 - sig))).astype(BF)
            gu[2 * j + 1, dst, :] = (hg * (g * sig)).astype(BF)

        for t in range(2):
            for k in (2, 1, 3):
                b_copy(2 * j + t, k).start()

    def ring(step, job, par, sign, first, slots, ssem, rsem, hops, dot):
        dest = zmod(z + sign * (hops - step))
        val = dot(dest)
        if step == 0:
            src = first.at[par]
        else:
            src = slots.at[job, step - 1]
            prev = first.at[par] if step == 1 else slots.at[job, step - 2]
            rc(prev, src, ssem.at[par, step - 1], rsem.at[job, step - 1], zdev(z + sign)).wait()
            val += src[...].astype(F32)
        src[...] = val.astype(BF)
        rc(src, slots.at[job, step], ssem.at[par, step], rsem.at[job, step],
           zdev(z + sign)).start()

    def ring_end(job, par, sign, slots_l, slots_h, lss, lrs, hss, hrs, dot):
        val = dot(z)
        last = slots_l.at[job, 3]
        rc(slots_l.at[job, 2], last, lss.at[par, 3], lrs.at[job, 3], zdev(z + sign)).wait()
        val += last[...].astype(F32)
        last = slots_h.at[job, 2]
        rc(slots_h.at[job, 1], last, hss.at[par, 2], hrs.at[job, 2], zdev(z - sign)).wait()
        return val + last[...].astype(F32)

    def down_dot(k):
        def dot(dest):
            return dot_nn(ht_all[rows_of(dest, UR), :], do_all[:, rows_of(k, DC)])
        return dot

    own_u = rows_of(xl, 224)
    other_u = rows_of(1 - xl, 224)

    def dx_copy(k):
        return rc(xsd.at[k], xrd.at[k], dx_ss.at[k], dx_rs.at[k], xdev)

    def down_step(step):
        @pl.loop(0, DK)
        def _(k):
            sign = 1 - 2 * lax.rem(k, 2)
            ring(step, k, k, sign, s0d.at[0], rld, dl_ss, dl_rs, 4, down_dot(k))
            if step < 3:
                ring(step, k, k, -sign, s0d.at[1], rsd, dh_ss, dh_rs, 3, down_dot(k))

    def down_end():
        @pl.loop(0, DK)
        def _(k):
            sign = 1 - 2 * lax.rem(k, 2)
            find[...] = ring_end(k, k, sign, rld, rsd, dl_ss, dl_rs, dh_ss, dh_rs, down_dot(k))
            accd[k] = find[own_u, :]
            xsd[k] = find[other_u, :].astype(BF)
            dx_copy(k).start()

    def da_out(i):
        return lc(dab.at[i], (nd, ndm, ndv)[i], da_sem.at[i])

    def down_update():
        lc(wd.at[rows_of(d, 224), :], dab.at[0], da_sem.at[0]).wait()
        lc(dm, dab.at[1], da_sem.at[1]).wait()
        lc(dv, dab.at[2], da_sem.at[2]).wait()

        @pl.loop(0, DK)
        def _(k):
            dx_copy(k).wait()
            cols = rows_of(k, DC)

            @pl.loop(0, 7)
            def _(i):
                sub = rows_of(i, 32)
                grad = accd[k, sub, :] + xrd[k, sub, :].astype(F32)
                new = adamw(dab[0, sub, cols], dab[1, sub, cols], dab[2, sub, cols], grad)
                for n in range(3):
                    dab[n, sub, cols] = new[n]

        for i in range(3):
            da_out(i).start()

    def gu_dot(q):
        def dot(dest):
            return dot_nn(xt_all[rows_of(dest, ZR), :], gu[q])
        return dot

    own_w = rows_of(xl, 64)
    other_w = rows_of(1 - xl, 64)

    def x_copy(q):
        par = lax.rem(q, 2)
        return rc(xs.at[par], xr.at[q], x_ss.at[par], x_rs.at[q], xdev)

    def ab_copies(q, par, out):
        cols = rows_of(lax.div(q, 2), CB)
        for t in range(2):
            refs = ((ng, ngm, ngv), (nu, num, nuv))[t] if out else ((wg, gm, gv), (wu, um, uv))[t]

            @pl.when(par == t)
            def _():
                for n in range(3):
                    if out:
                        lc(abuf.at[t, n], refs[n].at[:, cols], ob_sem.at[t, n]).start()
                    elif n == 0:
                        lc(refs[0].at[rows_of(d, 64), cols], abuf.at[t, n], ab_sem.at[t, n]).start()
                    else:
                        lc(refs[n].at[:, cols], abuf.at[t, n], ab_sem.at[t, n]).start()

    def ob_wait(par):
        for n in range(3):
            lc(abuf.at[par, n], ng.at[:, pl.ds(0, CB)], ob_sem.at[par, n]).wait()

    def gu_step(step, q):
        par = lax.rem(q, 2)
        sign = 1 - 2 * par
        ring(step, q, par, sign, s0.at[0], rl, l_ss, l_rs, 4, gu_dot(q))
        if step < 3:
            ring(step, q, par, -sign, s0.at[1], rs, h_ss, h_rs, 3, gu_dot(q))

    def gu_end(q):
        par = lax.rem(q, 2)

        @pl.when(q >= 2)
        def _():
            ob_wait(par)

        ab_copies(q, par, False)
        sign = 1 - 2 * par
        fin[...] = ring_end(q, par, sign, rl, rs, l_ss, l_rs, h_ss, h_rs, gu_dot(q))
        xs[par] = fin[other_w, :].astype(BF)
        x_copy(q).start()
        acc[par] = fin[own_w, :]

    def gu_update(q):
        par = lax.rem(q, 2)
        for n in range(3):
            lc(gm.at[:, pl.ds(0, CB)], abuf.at[par, n], ab_sem.at[par, n]).wait()
        x_copy(q).wait()

        @pl.loop(0, 4)
        def _(i):
            sub = rows_of(i, 16)
            grad = acc[par, sub, :] + xr[q, sub, :].astype(F32)
            new = adamw(abuf[par, 0, sub, :], abuf[par, 1, sub, :], abuf[par, 2, sub, :], grad)
            for n in range(3):
                abuf[par, n, sub, :] = new[n]

        ab_copies(q, par, True)

    def ig_add(q):
        par = lax.rem(q, 2)
        lc(wg.at[:, pl.ds(0, CB)], wgb.at[par], wg_sem.at[par]).wait()

        @pl.loop(0, 4)
        def _(i):
            sub = rows_of(i, 128)
            val = dot_nt(gu[q, sub, :], wgb[par])

            @pl.when(q == 0)
            def _():
                igacc[sub, :] = val

            @pl.when(q > 0)
            def _():
                igacc[sub, :] += val

        @pl.when(q + 2 < NQ)
        def _():
            wg_start(q + 2, par)

    def ig_copy(k):
        return rc(igs.at[k - 1], igr.at[k - 1], ig_ss.at[k - 1], ig_rs.at[k - 1], cdev(k))

    def ig_send():
        for k in (2, 1, 3):
            igs[k - 1] = igacc[rows_of(lax.rem(c + k, 4), 128), :].astype(BF)
            ig_copy(k).start()

    def ig_end():
        for k in (2, 1, 3):
            ig_copy(k).wait()
        val = igacc[own_c, :]
        for k in range(3):
            val += igr[k].astype(F32)
        igo[...] = val.astype(BF)
        lc(igo, ig_out, igo_sem).start()

    def ht_wait(*blocks):
        for i in blocks:
            for k in (2, 1, 3):
                ht_copy(i, k).wait_recv()

    for k in (2, 1, 3):
        do_copy(k).wait()

    @pl.loop(0, 4)
    def _(i):
        stage_a(i)

        @pl.when(i >= 1)
        def _():
            stage_b(i - 1)

        for step, blocks in enumerate(((0, 1, 2), (3, 4), (5, 6), (7,))):
            @pl.when(i == step)
            def _():
                ht_wait(*blocks)
                down_step(step)

    for k in (2, 1, 3):
        xt_copy(k).wait()

    @pl.loop(0, NQ + 5)
    def _(t):
        for step in (3, 2, 1, 0):
            q = t - step

            @pl.when((q >= 0) & (q < NQ))
            def _():
                if step == 0:
                    for k in (2, 1, 3):
                        b_copy(q, k).wait_recv()
                gu_step(step, q)

        half = lax.div(t, 2)

        @pl.when((lax.rem(t, 2) == 0) & (half + 4 < NB))
        def _():
            stage_a(half + 4)

        @pl.when((lax.rem(t, 2) == 1) & (half + 3 < NB))
        def _():
            stage_b(half + 3)

        @pl.when((t >= 4) & (t - 4 < NQ))
        def _():
            gu_end(t - 4)

        @pl.when(t >= 5)
        def _():
            gu_update(t - 5)

        @pl.when(t < NQ)
        def _():
            ig_add(t)

        @pl.when(t == 1)
        def _():
            down_end()

        @pl.when(t == 2)
        def _():
            down_update()

        @pl.when(t == NQ)
        def _():
            ig_send()

        @pl.when(t == NQ + 3)
        def _():
            ig_end()

    for i in range(3):
        da_out(i).wait()
    lc(igo, ig_out, igo_sem).wait()
    for par in range(2):
        ob_wait(par)
        for k in (2, 1, 3):
            a_copy(0, par, k).wait_send()

    @pl.loop(0, NZ)
    def _(i):
        for k in (2, 1, 3):
            ht_copy(i, k).wait_send()

    @pl.loop(0, NQ)
    def _(q):
        for k in (2, 1, 3):
            b_copy(q, k).wait_send()


def on_device(*args):
    vm = pltpu.VMEM
    dma = pltpu.SemaphoreType.DMA
    scratch = [
        vm((512, 1024), BF),
        vm((1024, 512), BF),
        vm((3584, 512), BF),
        vm((NQ, 512, CB), BF),
        vm((2, CB, 1024), BF),
        vm((2, 1024, CB), BF),
        vm((2, 3, 128, CB), BF),
        vm((2, 128, CB), F32),
        vm((NB, 3, 128, CB), BF),
        vm((2, 2, ZR, CB), BF),
        vm((NQ, 4, ZR, CB), BF),
        vm((NQ, 3, ZR, CB), BF),
        vm((ZR, CB), F32),
        vm((2, 64, CB), F32),
        vm((2, 64, CB), BF),
        vm((NQ, 64, CB), BF),
        vm((2, 3, 64, CB), BF),
        vm((2, DK, UR, DC), BF),
        vm((DK, 4, UR, DC), BF),
        vm((DK, 3, UR, DC), BF),
        vm((UR, DC), F32),
        vm((DK, 224, DC), F32),
        vm((DK, 224, DC), BF),
        vm((DK, 224, DC), BF),
        vm((3, 224, 1024), BF),
        vm((512, 1024), F32),
        vm((3, 128, 1024), BF),
        vm((3, 128, 1024), BF),
        vm((128, 1024), BF),
        dma((3,)), dma((3,)), dma((3,)), dma((3,)),
        dma((NZ, 3)), dma((NZ, 3)),
        dma((2, 3)), dma((NB, 3)),
        dma((NQ, 3)), dma((NQ, 3)),
        dma((2, 4)), dma((NQ, 4)),
        dma((2, 3)), dma((NQ, 3)),
        dma((2,)), dma((NQ,)),
        dma((DK, 4)), dma((DK, 4)),
        dma((DK, 3)), dma((DK, 3)),
        dma((DK,)), dma((DK,)),
        dma((3,)), dma((3,)),
        dma((2,)), dma((2,)), dma((2, 3)), dma((2, 3)), dma((3,)), dma(()),
    ]
    shapes = [(128, 1024)] + [(64, 3584)] * 6 + [(224, 1024)] * 3
    in_vmem = pl.BlockSpec(memory_space=pltpu.VMEM)
    in_any = pl.BlockSpec(memory_space=pl.ANY)
    return pl.pallas_call(
        kernel,
        out_shape=[jax.ShapeDtypeStruct(s, BF) for s in shapes],
        in_specs=[in_vmem] * 4 + [in_any] * 9,
        out_specs=[in_any] * 10,
        scratch_shapes=scratch,
        compiler_params=pltpu.CompilerParams(
            collective_id=0, has_side_effects=True, vmem_limit_bytes=60 * 2**20
        ),
        cost_estimate=pl.CostEstimate(
            flops=22548578304, bytes_accessed=34000000, transcendentals=4000000
        ),
    )(*args)


def solution(mesh):
    act = P(("depth", "col"), "row")
    pre = P(("depth", "row"), "col")
    wide = P("row", "col")
    tall = P("col", "row")
    wide_own = P(("row", "depth"), "col")
    tall_own = P(("col", "depth"), "row")
    return jax.shard_map(
        on_device,
        mesh=mesh,
        in_specs=(act, act, pre, pre, wide, wide, tall) + (wide_own,) * 4 + (tall_own,) * 2,
        out_specs=(act,) + (wide_own,) * 6 + (tall_own,) * 3,
        check_vma=False,
    )
```

```python
import jax
import jax.numpy as jnp
from jax import lax
from jax.experimental import pallas as pl
from jax.experimental.pallas import tpu as pltpu
from jax.sharding import PartitionSpec as P

BF = jnp.bfloat16
F32 = jnp.float32
MESH = pl.DeviceIdType.MESH

lr_rate = 0.0003
beta_one = 0.9
beta_two = 0.95
decay_rate = 0.1
eps_value = 1e-08
correct_one = 1.0 - 0.9**20
correct_two = 1.0 - 0.95**20

NZ = 8
CB = 512
NB = 7
NQ = 2 * NB
ZR = 128
UR = 448
DK = 2
DC = 256


def adamw(weight, first, second, grad):
    first_new = beta_one * first.astype(F32) + (1.0 - beta_one) * grad
    second_new = beta_two * second.astype(F32) + (1.0 - beta_two) * grad * grad
    wval = weight.astype(F32)
    step_val = (
        first_new / correct_one / (jnp.sqrt(second_new / correct_two) + eps_value)
        + decay_rate * wval
    )
    return (
        (wval - lr_rate * step_val).astype(BF),
        first_new.astype(BF),
        second_new.astype(BF),
    )


def dot_nn(a, b):
    return lax.dot_general(a, b, (((1,), (0,)), ((), ())), preferred_element_type=F32)


def dot_nt(a, b):
    return lax.dot_general(a, b, (((1,), (1,)), ((), ())), preferred_element_type=F32)


def rows_of(index, size):
    return pl.ds(pl.multiple_of(index * size, size), size)


def kernel(
    x_ref, do_ref, gp_ref, up_ref, wg, wu, wd, gm, gv, um, uv, dm, dv,
    ig_out, ng, ngm, ngv, nu, num, nuv, nd, ndm, ndv,
    do_all, xt_all, ht_all, gu, wdb, wgb, a_s, a_own, a_r,
    s0, rl, rs, fin, acc, xs, xr, abuf, s0x, rlx, rsx, xps, xpr,
    s0d, rld, rsd, find, accd, xsd, xrd, dab, s0dx, rldx, rsdx, xpsd, xprd,
    igacc, igs, igr, igo,
    do_ss, do_rs, xt_ss, xt_rs, ht_ss, ht_rs, a_ss, a_rs, b_ss, b_rs,
    l_ss, l_rs, h_ss, h_rs, x_ss, x_rs,
    lx_ss, lx_rs, hx_ss, hx_rs, xp_ss, xp_rs,
    dl_ss, dl_rs, dh_ss, dh_rs, dx_ss, dx_rs,
    dlx_ss, dlx_rs, dhx_ss, dhx_rs, dxp_ss, dxp_rs,
    ig_ss, ig_rs, wd_sem, wg_sem, ab_sem, ob_sem, da_sem, igo_sem,
):
    d = lax.axis_index("depth")
    r = lax.axis_index("row")
    c = lax.axis_index("col")
    z = lax.div(d, 2)
    xl = lax.rem(d, 2)

    def zmod(v):
        return lax.rem(v + 16, NZ)

    def zdev(v):
        return (2 * zmod(v) + xl, r, c)

    xdev = (2 * z + 1 - xl, r, c)

    def ydev(k):
        return (d, lax.rem(r + k, 4), c)

    def cdev(k):
        return (d, r, lax.rem(c + k, 4))

    def rc(src, dst, ss, rsem, dev):
        return pltpu.make_async_remote_copy(
            src_ref=src, dst_ref=dst, send_sem=ss, recv_sem=rsem,
            device_id=dev, device_id_type=MESH,
        )

    def lc(src, dst, sem):
        return pltpu.make_async_copy(src, dst, sem)

    def wd_copy(j, par):
        return lc(wd.at[rows_of(j, CB), :], wdb.at[par], wd_sem.at[par])

    def wg_start(q, par):
        cols = rows_of(lax.div(q, 2), CB)

        @pl.when(par == 0)
        def _():
            lc(wg.at[:, cols], wgb.at[0], wg_sem.at[0]).start()

        @pl.when(par == 1)
        def _():
            lc(wu.at[:, cols], wgb.at[1], wg_sem.at[1]).start()

    for p in range(2):
        wd_copy(p, p).start()
    lc(wg.at[:, pl.ds(0, CB)], wgb.at[0], wg_sem.at[0]).start()
    lc(wu.at[:, pl.ds(0, CB)], wgb.at[1], wg_sem.at[1]).start()
    lc(wd.at[rows_of(d, 224), :], dab.at[0], da_sem.at[0]).start()
    lc(dm, dab.at[1], da_sem.at[1]).start()
    lc(dv, dab.at[2], da_sem.at[2]).start()

    barrier = pltpu.get_barrier_semaphore()
    partners = [zdev(z + 1), zdev(z - 1), xdev]
    partners += [ydev(k) for k in (1, 2, 3)] + [cdev(k) for k in (1, 2, 3)]
    for dev in partners:
        pl.semaphore_signal(barrier, inc=1, device_id=dev, device_id_type=MESH)

    own_c = rows_of(c, 128)
    own_r = rows_of(r, 128)

    @pl.loop(0, NB)
    def _(j):
        cols = rows_of(j, CB)
        g = gp_ref[:, cols].astype(F32)
        h = g * jax.nn.sigmoid(g) * up_ref[:, cols].astype(F32)
        ht_all[cols, own_r] = h.T.astype(BF)

    pl.semaphore_wait(barrier, len(partners))

    c_far = lax.rem(c + 2, 4)
    c_near = c + 1 - 2 * lax.rem(c, 2)
    far_dev, near_dev = (d, r, c_far), (d, r, c_near)

    def do_copy(n):
        rows = own_c if n < 2 else rows_of(c_far, 128)
        view = do_all.at[rows, :]
        return rc(do_ref if n < 2 else view, view, do_ss.at[n], do_rs.at[n],
                  near_dev if n else far_dev)

    for n in range(2):
        do_copy(n).start()
    do_all[own_c, :] = do_ref[...]

    def row_dev(n):
        return ydev(3 if n % 2 else 1)

    def row_block(n):
        return rows_of(r if n < 2 else lax.rem(r + (1 if n % 2 else 3), 4), 128)

    def ht_copy(i, n):
        away = (2 * lax.rem(i, 2) - 1) * (4 - lax.div(i + 1, 2))
        first = zmod(z + away) * UR
        if n < 2:
            rows = pl.ds(pl.multiple_of(first, 64), UR)
        else:
            rows = pl.ds(pl.multiple_of(first + (n - 2) * 224, 32), 224)
        view = ht_all.at[rows, row_block(n)]
        return rc(view, view, ht_ss.at[i, n], ht_rs.at[i, n], row_dev(n))

    def ht_send(first, last):
        @pl.loop(first, last)
        def _(i):
            for n in range(2):
                ht_copy(i, n).start()

    def ht_pass(first, last):
        @pl.loop(first, last)
        def _(i):
            for n in range(2):
                ht_copy(i, n).wait_recv()
                ht_copy(i, n + 2).start()

    def ht_wait(first, last):
        @pl.loop(first, last)
        def _(i):
            for n in (2, 3):
                ht_copy(i, n).wait_recv()

    ht_send(0, 3)

    xt_all[:, own_c] = x_ref[...].T

    def xt_copy(n):
        view = xt_all.at[:, own_c if n < 2 else rows_of(c_far, 128)]
        return rc(view, view, xt_ss.at[n], xt_rs.at[n], near_dev if n else far_dev)

    for n in range(2):
        xt_copy(n).start()

    def a_copy(j, par, k):
        return rc(a_s.at[par, k - 1], a_r.at[j, k - 1], a_ss.at[par, k - 1],
                  a_rs.at[j, k - 1], ydev(k))

    def stage_a(j):
        par = lax.rem(j, 2)
        wd_copy(j, par).wait()

        @pl.when(j >= 2)
        def _():
            for k in (2, 1, 3):
                a_copy(j, par, k).wait_send()

        def part(k):
            return dot_nt(do_all[rows_of(lax.rem(r + k, 4), 128), :], wdb[par])

        for k in (2, 1, 3):
            a_s[par, k - 1] = part(k).astype(BF)
            a_copy(j, par, k).start()
        a_own[par] = part(0)

        @pl.when(j + 2 < NB)
        def _():
            wd_copy(j + 2, par).start()

    def b_copy(q, n):
        if n < 2:
            view = gu.at[q, row_block(n), :]
        else:
            first = lax.rem(r + (1 if n % 2 else 3), 4) * 128 + (n - 2) * 64
            view = gu.at[q, pl.ds(pl.multiple_of(first, 64), 64), :]
        return rc(view, view, b_ss.at[q, n], b_rs.at[q, n], row_dev(n))

    def pass_b(j):
        for t in range(2):
            for n in range(2):
                b_copy(2 * j + t, n).wait_recv()
                b_copy(2 * j + t, n + 2).start()

    def stage_b(j):
        par = lax.rem(j, 2)
        for k in (2, 1, 3):
            a_copy(j, par, k).wait_recv()

        @pl.loop(0, 8)
        def _(i):
            sub = rows_of(i, 16)
            cols = rows_of(j, CB)
            hg = a_own[par, sub, :]
            for k in range(3):
                hg += a_r[j, k, sub, :].astype(F32)
            g = gp_ref[sub, cols].astype(F32)
            u = up_ref[sub, cols].astype(F32)
            sig = jax.nn.sigmoid(g)
            dst = pl.ds(pl.multiple_of(r * 128 + i * 16, 16), 16)
            gu[2 * j, dst, :] = (hg * u * sig * (1.0 + g * (1.0 - sig))).astype(BF)
            gu[2 * j + 1, dst, :] = (hg * (g * sig)).astype(BF)

        for t in range(2):
            for n in range(2):
                b_copy(2 * j + t, n).start()

    def ring(step, job, par, sign, first, slots, ssem, rsem, hops, dot):
        dest = zmod(z + sign * (hops - step))
        val = dot(dest)
        if step == 0:
            src = first.at[par]
        else:
            src = slots.at[job, step - 1]
            prev = first.at[par] if step == 1 else slots.at[job, step - 2]
            rc(prev, src, ssem.at[par, step - 1], rsem.at[job, step - 1], zdev(z + sign)).wait()
            val += src[...].astype(F32)
        src[...] = val.astype(BF)
        rc(src, slots.at[job, step], ssem.at[par, step], rsem.at[job, step],
           zdev(z + sign)).start()

    def ring_end(job, par, sign, slots_l, slots_h, lss, lrs, hss, hrs, dot):
        val = dot(z)
        last = slots_l.at[job, 3]
        rc(slots_l.at[job, 2], last, lss.at[par, 3], lrs.at[job, 3], zdev(z + sign)).wait()
        val += last[...].astype(F32)
        last = slots_h.at[job, 2]
        rc(slots_h.at[job, 1], last, hss.at[par, 2], hrs.at[job, 2], zdev(z - sign)).wait()
        return val + last[...].astype(F32)

    def down_dot(k):
        def dot(dest):
            return dot_nn(ht_all[rows_of(dest, UR), :], do_all[:, rows_of(k, DC)])
        return dot

    own_u = rows_of(xl, 224)
    other_u = rows_of(1 - xl, 224)

    def half_dot(k, dest, side):
        rows = pl.ds(pl.multiple_of(dest * UR + side * 224, 32), 224)
        return dot_nn(ht_all[rows, :], do_all[:, rows_of(k + DK, DC)])

    def dxp_copy(k, dest):
        return rc(xpsd.at[k, dest], xprd.at[k, dest], dxp_ss.at[k, dest], dxp_rs.at[k, dest], xdev)

    def downx_pre(step):
        @pl.loop(0, DK)
        def _(k):
            sign = 1 - 2 * k
            dests = [zmod(z + sign * (4 - step))]
            if step < 3:
                dests.append(zmod(z - sign * (3 - step)))
            for dest in dests:
                xpsd[k, dest] = half_dot(k, dest, 1 - xl).astype(BF)
                dxp_copy(k, dest).start()

    def downx_dot(k):
        def dot(dest):
            val = half_dot(k, dest, xl)
            dxp_copy(k, dest).wait()
            return val + xprd[k, dest].astype(F32)
        return dot

    def dx_copy(k):
        return rc(xsd.at[k], xrd.at[k], dx_ss.at[k], dx_rs.at[k], xdev)

    def down_step(step):
        @pl.loop(0, DK)
        def _(k):
            sign = 1 - 2 * k
            ring(step, k, k, sign, s0d.at[0], rld, dl_ss, dl_rs, 4, down_dot(k))
            if step < 3:
                ring(step, k, k, -sign, s0d.at[1], rsd, dh_ss, dh_rs, 3, down_dot(k))

    def downx_step(step):
        @pl.loop(0, DK)
        def _(k):
            sign = 1 - 2 * k
            ring(step, k, k, sign, s0dx.at[0], rldx, dlx_ss, dlx_rs, 4, downx_dot(k))
            if step < 3:
                ring(step, k, k, -sign, s0dx.at[1], rsdx, dhx_ss, dhx_rs, 3, downx_dot(k))

    def down_end():
        @pl.loop(0, DK)
        def _(k):
            sign = 1 - 2 * k
            find[...] = ring_end(k, k, sign, rld, rsd, dl_ss, dl_rs, dh_ss, dh_rs, down_dot(k))
            xsd[k] = find[other_u, :].astype(BF)
            dx_copy(k).start()
            accd[k] = find[own_u, :]

        @pl.loop(0, DK)
        def _(k):
            sign = 1 - 2 * k
            accd[k + DK] = ring_end(
                k, k, sign, rldx, rsdx, dlx_ss, dlx_rs, dhx_ss, dhx_rs, downx_dot(k))

    def da_out(i):
        return lc(dab.at[i], (nd, ndm, ndv)[i], da_sem.at[i])

    def down_update():
        lc(wd.at[rows_of(d, 224), :], dab.at[0], da_sem.at[0]).wait()
        lc(dm, dab.at[1], da_sem.at[1]).wait()
        lc(dv, dab.at[2], da_sem.at[2]).wait()

        @pl.loop(0, DK)
        def _(k):
            dx_copy(k).wait()
            accd[k] += xrd[k].astype(F32)

        @pl.loop(0, 2 * DK)
        def _(k):
            cols = rows_of(k, DC)

            @pl.loop(0, 7)
            def _(i):
                sub = rows_of(i, 32)
                new = adamw(
                    dab[0, sub, cols], dab[1, sub, cols], dab[2, sub, cols], accd[k, sub, :])
                for n in range(3):
                    dab[n, sub, cols] = new[n]

        for i in range(3):
            da_out(i).start()

    def gate_dot(j):
        def dot(dest):
            return dot_nn(xt_all[rows_of(dest, ZR), :], gu[2 * j])
        return dot

    own_w = rows_of(xl, 64)
    other_w = rows_of(1 - xl, 64)

    def up_half(j, dest, side):
        rows = pl.ds(pl.multiple_of(dest * ZR + side * 64, 64), 64)
        return dot_nn(xt_all[rows, :], gu[2 * j + 1])

    def xp_copy(j, dest):
        par = lax.rem(j, 2)
        return rc(xps.at[par, dest], xpr.at[j, dest], xp_ss.at[par, dest], xp_rs.at[j, dest], xdev)

    def up_pre(j):
        par = lax.rem(j, 2)
        sign = 2 * par - 1

        @pl.loop(0, NZ)
        def _(i):
            away = sign * (1 - 2 * lax.rem(i, 2)) * (4 - lax.div(i + 1, 2))
            dest = zmod(z + away)

            @pl.when(j >= 2)
            def _():
                xp_copy(j, dest).wait_send()

            xps[par, dest] = up_half(j, dest, 1 - xl).astype(BF)
            xp_copy(j, dest).start()

    def up_dot(j):
        def dot(dest):
            val = up_half(j, dest, xl)
            xp_copy(j, dest).wait_recv()
            return val + xpr[j, dest].astype(F32)
        return dot

    def x_copy(j):
        par = lax.rem(j, 2)
        return rc(xs.at[par], xr.at[j], x_ss.at[par], x_rs.at[j], xdev)

    def ab_in(t, j):
        @pl.when(j >= 1)
        def _():
            ob_wait(t)

        cols = rows_of(j, CB)
        w, m, v = ((wg, gm, gv), (wu, um, uv))[t]
        lc(w.at[rows_of(d, 64), cols], abuf.at[t, 0], ab_sem.at[t, 0]).start()
        lc(m.at[:, cols], abuf.at[t, 1], ab_sem.at[t, 1]).start()
        lc(v.at[:, cols], abuf.at[t, 2], ab_sem.at[t, 2]).start()

    def ob_wait(t):
        for n in range(3):
            lc(abuf.at[t, n], ng.at[:, pl.ds(0, CB)], ob_sem.at[t, n]).wait()

    def gate_step(step, j):
        par = lax.rem(j, 2)
        sign = 1 - 2 * par
        ring(step, j, par, sign, s0.at[0], rl, l_ss, l_rs, 4, gate_dot(j))
        if step < 3:
            ring(step, j, par, -sign, s0.at[1], rs, h_ss, h_rs, 3, gate_dot(j))

    def up_step(step, j):
        par = lax.rem(j, 2)
        sign = 2 * par - 1
        ring(step, j, par, sign, s0x.at[0], rlx, lx_ss, lx_rs, 4, up_dot(j))
        if step < 3:
            ring(step, j, par, -sign, s0x.at[1], rsx, hx_ss, hx_rs, 3, up_dot(j))

    def gate_end(j):
        par = lax.rem(j, 2)
        fin[...] = ring_end(j, par, 1 - 2 * par, rl, rs, l_ss, l_rs, h_ss, h_rs, gate_dot(j))
        xs[par] = fin[other_w, :].astype(BF)
        x_copy(j).start()
        acc[par] = fin[own_w, :]

    def up_end(j):
        par = lax.rem(j, 2)
        acc[2] = ring_end(j, par, 2 * par - 1, rlx, rsx, lx_ss, lx_rs, hx_ss, hx_rs, up_dot(j))
        update(1, j, 2)

    def gate_update(j):
        x_copy(j).wait()
        par = lax.rem(j, 2)
        acc[par] += xr[j].astype(F32)
        update(0, j, par)

    def update(t, j, slot):
        for n in range(3):
            lc(gm.at[:, pl.ds(0, CB)], abuf.at[t, n], ab_sem.at[t, n]).wait()

        @pl.loop(0, 4)
        def _(i):
            sub = rows_of(i, 16)
            new = adamw(abuf[t, 0, sub, :], abuf[t, 1, sub, :], abuf[t, 2, sub, :], acc[slot, sub, :])
            for n in range(3):
                abuf[t, n, sub, :] = new[n]

        cols = rows_of(j, CB)
        refs = ((ng, ngm, ngv), (nu, num, nuv))[t]
        for n in range(3):
            lc(abuf.at[t, n], refs[n].at[:, cols], ob_sem.at[t, n]).start()

    def ig_add(q):
        par = lax.rem(q, 2)
        lc(wg.at[:, pl.ds(0, CB)], wgb.at[par], wg_sem.at[par]).wait()

        @pl.loop(0, 4)
        def _(i):
            sub = rows_of(i, 128)
            val = dot_nt(gu[q, sub, :], wgb[par])

            @pl.when(q == 0)
            def _():
                igacc[sub, :] = val

            @pl.when(q > 0)
            def _():
                igacc[sub, :] += val

        @pl.when(q + 2 < NQ)
        def _():
            wg_start(q + 2, par)

    def ig_copy(k):
        return rc(igs.at[k - 1], igr.at[k - 1], ig_ss.at[k - 1], ig_rs.at[k - 1], cdev(k))

    def ig_send():
        for k in (2, 1, 3):
            igs[k - 1] = igacc[rows_of(lax.rem(c + k, 4), 128), :].astype(BF)
            ig_copy(k).start()

    def ig_end():
        for k in (2, 1, 3):
            ig_copy(k).wait()
        val = igacc[own_c, :]
        for k in range(3):
            val += igr[k].astype(F32)
        igo[...] = val.astype(BF)
        lc(igo, ig_out, igo_sem).start()

    def relayed(copy):
        copy(0).wait_recv()
        copy(2).start()
        copy(0).wait_send()
        copy(1).wait()
        copy(2).wait()

    ht_pass(0, 3)
    relayed(do_copy)
    stage_a(0)
    ht_send(3, 5)
    ht_wait(0, 3)
    downx_pre(0)
    down_step(0)
    downx_step(0)

    ht_pass(3, 5)
    stage_a(1)
    ht_send(5, 7)
    ht_wait(3, 5)
    downx_pre(1)
    down_step(1)
    downx_step(1)

    ht_pass(5, 7)
    stage_b(0)
    ht_send(7, 8)
    ht_wait(5, 7)
    downx_pre(2)
    down_step(2)
    downx_step(2)

    stage_a(2)
    ht_pass(7, 8)
    pass_b(0)
    stage_b(1)
    ht_wait(7, 8)
    downx_pre(3)
    downx_pre(4)
    down_step(3)
    downx_step(3)
    relayed(xt_copy)

    def up_gate_ready(q):
        for n in (2, 3):
            b_copy(q, n).wait_recv()

    @pl.loop(0, NQ + 4)
    def _(t):
        for step in (3, 2, 1, 0):
            q = t - step
            job = lax.div(q, 2)

            @pl.when((q >= 0) & (q < NQ) & (lax.rem(q, 2) == 0))
            def _():
                if step == 0:
                    up_gate_ready(q)
                gate_step(step, job)

            @pl.when((q >= 0) & (q < NQ) & (lax.rem(q, 2) == 1))
            def _():
                if step == 3:
                    ab_in(1, job)
                up_step(step, job)

        @pl.when((t < NQ) & (lax.rem(t, 2) == 0))
        def _():
            up_gate_ready(t + 1)
            up_pre(lax.div(t, 2))

        half = lax.div(t, 2)

        @pl.when((lax.rem(t, 2) == 0) & (half + 1 < NB))
        def _():
            pass_b(half + 1)

        @pl.when((lax.rem(t, 2) == 0) & (half + 3 < NB))
        def _():
            stage_a(half + 3)

        @pl.when((lax.rem(t, 2) == 1) & (half + 2 < NB))
        def _():
            stage_b(half + 2)

        @pl.when((t >= 4) & (lax.rem(t, 2) == 0))
        def _():
            gate_end(lax.div(t - 4, 2))

        @pl.when((t >= 5) & (lax.rem(t, 2) == 1))
        def _():
            up_end(lax.div(t - 5, 2))

        @pl.when((t >= 7) & (lax.rem(t, 2) == 1))
        def _():
            gate_update(lax.div(t - 7, 2))

        @pl.when((t >= 5) & (lax.rem(t, 2) == 1))
        def _():
            ab_in(0, lax.div(t - 5, 2))

        @pl.when(t < NQ)
        def _():
            ig_add(t)

        @pl.when(t == 1)
        def _():
            down_end()

        @pl.when(t == 2)
        def _():
            down_update()

        @pl.when(t == NQ)
        def _():
            ig_send()

    gate_update(NB - 1)
    ig_end()
    for i in range(3):
        da_out(i).wait()
    lc(igo, ig_out, igo_sem).wait()
    for par in range(2):
        ob_wait(par)
        for k in (2, 1, 3):
            a_copy(0, par, k).wait_send()

    @pl.loop(0, NZ)
    def _(i):
        for n in range(4):
            ht_copy(i, n).wait_send()

    @pl.loop(0, NQ)
    def _(q):
        for n in range(4):
            b_copy(q, n).wait_send()

    @pl.loop(0, NZ)
    def _(i):
        for j in (NB - 2, NB - 1):
            xp_copy(j, i).wait_send()


def hand_over(*refs):
    src, dst, buf = refs[:10], refs[10:20], refs[20:30]
    ins = [pltpu.make_async_copy(src[i], buf[i], refs[30].at[i]) for i in range(10)]
    outs = [pltpu.make_async_copy(buf[i], dst[i], refs[31].at[i]) for i in range(10)]
    for copy in ins:
        copy.start()
    for i in range(10):
        ins[i].wait()
        outs[i].start()
    for copy in outs:
        copy.wait()


def on_device(*args):
    vm = pltpu.VMEM
    dma = pltpu.SemaphoreType.DMA
    scratch = [
        vm((512, 1024), BF),
        vm((1024, 512), BF),
        vm((3584, 512), BF),
        vm((NQ, 512, CB), BF),
        vm((2, CB, 1024), BF),
        vm((2, 1024, CB), BF),
        vm((2, 3, 128, CB), BF),
        vm((2, 128, CB), F32),
        vm((NB, 3, 128, CB), BF),
        vm((2, 2, ZR, CB), BF),
        vm((NB, 4, ZR, CB), BF),
        vm((NB, 3, ZR, CB), BF),
        vm((ZR, CB), F32),
        vm((3, 64, CB), F32),
        vm((2, 64, CB), BF),
        vm((NB, 64, CB), BF),
        vm((2, 3, 64, CB), BF),
        vm((2, 2, 64, CB), BF),
        vm((NB, 4, 64, CB), BF),
        vm((NB, 3, 64, CB), BF),
        vm((2, NZ, 64, CB), BF),
        vm((NB, NZ, 64, CB), BF),
        vm((2, DK, UR, DC), BF),
        vm((DK, 4, UR, DC), BF),
        vm((DK, 3, UR, DC), BF),
        vm((UR, DC), F32),
        vm((2 * DK, 224, DC), F32),
        vm((DK, 224, DC), BF),
        vm((DK, 224, DC), BF),
        vm((3, 224, 1024), BF),
        vm((2, DK, 224, DC), BF),
        vm((DK, 4, 224, DC), BF),
        vm((DK, 3, 224, DC), BF),
        vm((DK, NZ, 224, DC), BF),
        vm((DK, NZ, 224, DC), BF),
        vm((512, 1024), F32),
        vm((3, 128, 1024), BF),
        vm((3, 128, 1024), BF),
        vm((128, 1024), BF),
        dma((3,)), dma((3,)), dma((3,)), dma((3,)),
        dma((NZ, 4)), dma((NZ, 4)),
        dma((2, 3)), dma((NB, 3)),
        dma((NQ, 4)), dma((NQ, 4)),
        dma((2, 4)), dma((NB, 4)), dma((2, 3)), dma((NB, 3)),
        dma((2,)), dma((NB,)),
        dma((2, 4)), dma((NB, 4)), dma((2, 3)), dma((NB, 3)),
        dma((2, NZ)), dma((NB, NZ)),
        dma((DK, 4)), dma((DK, 4)), dma((DK, 3)), dma((DK, 3)),
        dma((DK,)), dma((DK,)),
        dma((DK, 4)), dma((DK, 4)), dma((DK, 3)), dma((DK, 3)),
        dma((DK, NZ)), dma((DK, NZ)),
        dma((3,)), dma((3,)),
        dma((2,)), dma((2,)), dma((2, 3)), dma((2, 3)), dma((3,)), dma(()),
    ]
    shapes = [(128, 1024)] + [(64, 3584)] * 6 + [(224, 1024)] * 3
    in_vmem = pl.BlockSpec(memory_space=pltpu.VMEM)
    in_any = pl.BlockSpec(memory_space=pl.ANY)
    shapes = [jax.ShapeDtypeStruct(s, BF) for s in shapes]
    results = pl.pallas_call(
        kernel,
        out_shape=shapes,
        in_specs=[in_vmem] * 4 + [in_any] * 9,
        out_specs=[in_any] * 10,
        scratch_shapes=scratch,
        compiler_params=pltpu.CompilerParams(
            collective_id=0, has_side_effects=True, vmem_limit_bytes=60 * 2**20
        ),
        cost_estimate=pl.CostEstimate(
            flops=22548578304, bytes_accessed=34000000, transcendentals=4000000
        ),
    )(*args)
    return pl.pallas_call(
        hand_over,
        out_shape=shapes,
        in_specs=[in_any] * 10,
        out_specs=[in_any] * 10,
        scratch_shapes=[vm(s.shape, BF) for s in shapes] + [dma((10,)), dma((10,))],
    )(*results)


def solution(mesh):
    act = P(("depth", "col"), "row")
    pre = P(("depth", "row"), "col")
    wide = P("row", "col")
    tall = P("col", "row")
    wide_own = P(("row", "depth"), "col")
    tall_own = P(("col", "depth"), "row")
    return jax.shard_map(
        on_device,
        mesh=mesh,
        in_specs=(act, act, pre, pre, wide, wide, tall) + (wide_own,) * 4 + (tall_own,) * 2,
        out_specs=(act,) + (wide_own,) * 6 + (tall_own,) * 3,
        check_vma=False,
    )
```

```python
import jax
import jax.numpy as jnp
from jax import lax
from jax.experimental import pallas as pl
from jax.experimental.pallas import tpu as pltpu
from jax.sharding import PartitionSpec as P

BF = jnp.bfloat16
F32 = jnp.float32
MESH = pl.DeviceIdType.MESH

lr_rate = 0.0003
beta_one = 0.9
beta_two = 0.95
decay_rate = 0.1
eps_value = 1e-08
correct_one = 1.0 - 0.9**20
correct_two = 1.0 - 0.95**20

NZ = 8
CB = 512
NB = 7
NQ = 2 * NB
ZR = 128
UR = 448
DK = 2
DC = 256


def adamw(weight, first, second, grad):
    first_new = beta_one * first.astype(F32) + (1.0 - beta_one) * grad
    second_new = beta_two * second.astype(F32) + (1.0 - beta_two) * grad * grad
    wval = weight.astype(F32)
    step_val = (
        first_new / correct_one / (jnp.sqrt(second_new / correct_two) + eps_value)
        + decay_rate * wval
    )
    return (
        (wval - lr_rate * step_val).astype(BF),
        first_new.astype(BF),
        second_new.astype(BF),
    )


def dot_nn(a, b):
    return lax.dot_general(a, b, (((1,), (0,)), ((), ())), preferred_element_type=F32)


def dot_nt(a, b):
    return lax.dot_general(a, b, (((1,), (1,)), ((), ())), preferred_element_type=F32)


def rows_of(index, size):
    return pl.ds(pl.multiple_of(index * size, size), size)


def kernel(
    x_ref, do_ref, gp_ref, up_ref, wg, wu, wd, gm, gv, um, uv, dm, dv,
    ig_out, ng, ngm, ngv, nu, num, nuv, nd, ndm, ndv,
    do_all, xt_all, ht_all, gu, wdb, wgb, a_s, a_own, a_r,
    s0, rl, rs, fin, acc, xs, xr, abuf, s0x, rlx, rsx, xps, xpr,
    s0d, rld, rsd, find, accd, xsd, xrd, dab, s0dx, rldx, rsdx, xpsd, xprd,
    igacc, igs, igr, igo,
    do_ss, do_rs, xt_ss, xt_rs, ht_ss, ht_rs, a_ss, a_rs, b_ss, b_rs,
    l_ss, l_rs, h_ss, h_rs, x_ss, x_rs,
    lx_ss, lx_rs, hx_ss, hx_rs, xp_ss, xp_rs,
    dl_ss, dl_rs, dh_ss, dh_rs, dx_ss, dx_rs,
    dlx_ss, dlx_rs, dhx_ss, dhx_rs, dxp_ss, dxp_rs,
    ig_ss, ig_rs, wd_sem, wg_sem, ab_sem, ob_sem, da_sem, igo_sem,
):
    d = lax.axis_index("depth")
    r = lax.axis_index("row")
    c = lax.axis_index("col")
    z = lax.div(d, 2)
    xl = lax.rem(d, 2)

    def zmod(v):
        return lax.rem(v + 16, NZ)

    def zdev(v):
        return (2 * zmod(v) + xl, r, c)

    xdev = (2 * z + 1 - xl, r, c)

    def ydev(k):
        return (d, lax.rem(r + k, 4), c)

    def cdev(k):
        return (d, r, lax.rem(c + k, 4))

    def rc(src, dst, ss, rsem, dev):
        return pltpu.make_async_remote_copy(
            src_ref=src, dst_ref=dst, send_sem=ss, recv_sem=rsem,
            device_id=dev, device_id_type=MESH,
        )

    def lc(src, dst, sem):
        return pltpu.make_async_copy(src, dst, sem)

    def wd_copy(j, par):
        return lc(wd.at[rows_of(j, CB), :], wdb.at[par], wd_sem.at[par])

    def wg_start(q, par):
        cols = rows_of(lax.div(q, 2), CB)

        @pl.when(par == 0)
        def _():
            lc(wg.at[:, cols], wgb.at[0], wg_sem.at[0]).start()

        @pl.when(par == 1)
        def _():
            lc(wu.at[:, cols], wgb.at[1], wg_sem.at[1]).start()

    for p in range(2):
        wd_copy(p, p).start()
    lc(wg.at[:, pl.ds(0, CB)], wgb.at[0], wg_sem.at[0]).start()
    lc(wu.at[:, pl.ds(0, CB)], wgb.at[1], wg_sem.at[1]).start()
    lc(wd.at[rows_of(d, 224), :], dab.at[0], da_sem.at[0]).start()
    lc(dm, dab.at[1], da_sem.at[1]).start()
    lc(dv, dab.at[2], da_sem.at[2]).start()

    barrier = pltpu.get_barrier_semaphore()
    partners = [zdev(z + 1), zdev(z - 1), xdev]
    partners += [ydev(k) for k in (1, 2, 3)] + [cdev(k) for k in (1, 2, 3)]
    for dev in partners:
        pl.semaphore_signal(barrier, inc=1, device_id=dev, device_id_type=MESH)

    own_c = rows_of(c, 128)
    own_r = rows_of(r, 128)

    @pl.loop(0, NB)
    def _(j):
        cols = rows_of(j, CB)
        g = gp_ref[:, cols].astype(F32)
        h = g * jax.nn.sigmoid(g) * up_ref[:, cols].astype(F32)
        ht_all[cols, own_r] = h.T.astype(BF)

    pl.semaphore_wait(barrier, len(partners))

    c_far = lax.rem(c + 2, 4)
    c_near = c + 1 - 2 * lax.rem(c, 2)
    far_dev, near_dev = (d, r, c_far), (d, r, c_near)

    def do_copy(n):
        rows = own_c if n < 2 else rows_of(c_far, 128)
        view = do_all.at[rows, :]
        return rc(do_ref if n < 2 else view, view, do_ss.at[n], do_rs.at[n],
                  near_dev if n else far_dev)

    for n in range(2):
        do_copy(n).start()
    do_all[own_c, :] = do_ref[...]

    def row_dev(n):
        return ydev(3 if n % 2 else 1)

    def row_block(n):
        return rows_of(r if n < 2 else lax.rem(r + (1 if n % 2 else 3), 4), 128)

    def ht_copy(i, n):
        away = (2 * lax.rem(i, 2) - 1) * (4 - lax.div(i + 1, 2))
        first = zmod(z + away) * UR
        if n < 2:
            rows = pl.ds(pl.multiple_of(first, 64), UR)
        else:
            rows = pl.ds(pl.multiple_of(first + (n - 2) * 224, 32), 224)
        view = ht_all.at[rows, row_block(n)]
        return rc(view, view, ht_ss.at[i, n], ht_rs.at[i, n], row_dev(n))

    def ht_send(first, last):
        @pl.loop(first, last)
        def _(i):
            for n in range(2):
                ht_copy(i, n).start()

    def ht_pass(first, last):
        @pl.loop(first, last)
        def _(i):
            for n in range(2):
                ht_copy(i, n).wait_recv()
                ht_copy(i, n + 2).start()

    def ht_wait(first, last):
        @pl.loop(first, last)
        def _(i):
            for n in (2, 3):
                ht_copy(i, n).wait_recv()

    ht_send(0, 3)

    xt_all[:, own_c] = x_ref[...].T

    def xt_copy(n):
        view = xt_all.at[:, own_c if n < 2 else rows_of(c_far, 128)]
        return rc(view, view, xt_ss.at[n], xt_rs.at[n], near_dev if n else far_dev)

    def a_copy(j, par, k):
        return rc(a_s.at[par, k - 1], a_r.at[j, k - 1], a_ss.at[par, k - 1],
                  a_rs.at[j, k - 1], ydev(k))

    def stage_a(j):
        par = lax.rem(j, 2)
        wd_copy(j, par).wait()

        @pl.when(j >= 2)
        def _():
            for k in (2, 1, 3):
                a_copy(j, par, k).wait_send()

        def part(k):
            return dot_nt(do_all[rows_of(lax.rem(r + k, 4), 128), :], wdb[par])

        for k in (2, 1, 3):
            a_s[par, k - 1] = part(k).astype(BF)
            a_copy(j, par, k).start()
        a_own[par] = part(0)

        @pl.when(j + 2 < NB)
        def _():
            wd_copy(j + 2, par).start()

    def b_copy(q, n):
        if n < 2:
            view = gu.at[q, row_block(n), :]
        else:
            first = lax.rem(r + (1 if n % 2 else 3), 4) * 128 + (n - 2) * 64
            view = gu.at[q, pl.ds(pl.multiple_of(first, 64), 64), :]
        return rc(view, view, b_ss.at[q, n], b_rs.at[q, n], row_dev(n))

    def pass_b(j):
        for t in range(2):
            for n in range(2):
                b_copy(2 * j + t, n).wait_recv()
                b_copy(2 * j + t, n + 2).start()

    def stage_b(j):
        par = lax.rem(j, 2)
        for k in (2, 1, 3):
            a_copy(j, par, k).wait_recv()

        @pl.loop(0, 8)
        def _(i):
            sub = rows_of(i, 16)
            cols = rows_of(j, CB)
            hg = a_own[par, sub, :]
            for k in range(3):
                hg += a_r[j, k, sub, :].astype(F32)
            g = gp_ref[sub, cols].astype(F32)
            u = up_ref[sub, cols].astype(F32)
            sig = jax.nn.sigmoid(g)
            dst = pl.ds(pl.multiple_of(r * 128 + i * 16, 16), 16)
            gu[2 * j, dst, :] = (hg * u * sig * (1.0 + g * (1.0 - sig))).astype(BF)
            gu[2 * j + 1, dst, :] = (hg * (g * sig)).astype(BF)

        for t in range(2):
            for n in range(2):
                b_copy(2 * j + t, n).start()

    def ring(step, job, par, sign, first, slots, ssem, rsem, hops, dot):
        dest = zmod(z + sign * (hops - step))
        val = dot(dest)
        if step == 0:
            src = first.at[par]
        else:
            src = slots.at[job, step - 1]
            prev = first.at[par] if step == 1 else slots.at[job, step - 2]
            rc(prev, src, ssem.at[par, step - 1], rsem.at[job, step - 1], zdev(z + sign)).wait()
            val += src[...].astype(F32)
        src[...] = val.astype(BF)
        rc(src, slots.at[job, step], ssem.at[par, step], rsem.at[job, step],
           zdev(z + sign)).start()

    def ring_end(job, par, sign, slots_l, slots_h, lss, lrs, hss, hrs, dot):
        val = dot(z)
        last = slots_l.at[job, 3]
        rc(slots_l.at[job, 2], last, lss.at[par, 3], lrs.at[job, 3], zdev(z + sign)).wait()
        val += last[...].astype(F32)
        last = slots_h.at[job, 2]
        rc(slots_h.at[job, 1], last, hss.at[par, 2], hrs.at[job, 2], zdev(z - sign)).wait()
        return val + last[...].astype(F32)

    def down_dot(k):
        def dot(dest):
            return dot_nn(ht_all[rows_of(dest, UR), :], do_all[:, rows_of(k, DC)])
        return dot

    own_u = rows_of(xl, 224)
    other_u = rows_of(1 - xl, 224)

    def half_dot(k, dest, side):
        rows = pl.ds(pl.multiple_of(dest * UR + side * 224, 32), 224)
        return dot_nn(ht_all[rows, :], do_all[:, rows_of(k + DK, DC)])

    def dxp_copy(k, dest):
        return rc(xpsd.at[k, dest], xprd.at[k, dest], dxp_ss.at[k, dest], dxp_rs.at[k, dest], xdev)

    def downx_pre(step, ways="lh"):
        @pl.loop(0, DK)
        def _(k):
            sign = 1 - 2 * k
            dests = []
            if "l" in ways:
                dests.append(zmod(z + sign * (4 - step)))
            if "h" in ways and step < 3:
                dests.append(zmod(z - sign * (3 - step)))
            for dest in dests:
                xpsd[k, dest] = half_dot(k, dest, 1 - xl).astype(BF)
                dxp_copy(k, dest).start()

    def downx_dot(k):
        def dot(dest):
            val = half_dot(k, dest, xl)
            dxp_copy(k, dest).wait()
            return val + xprd[k, dest].astype(F32)
        return dot

    def dx_copy(k):
        return rc(xsd.at[k], xrd.at[k], dx_ss.at[k], dx_rs.at[k], xdev)

    def down_step(step, ways="lh"):
        @pl.loop(0, DK)
        def _(k):
            sign = 1 - 2 * k
            if "l" in ways:
                ring(step, k, k, sign, s0d.at[0], rld, dl_ss, dl_rs, 4, down_dot(k))
            if "h" in ways and step < 3:
                ring(step, k, k, -sign, s0d.at[1], rsd, dh_ss, dh_rs, 3, down_dot(k))

    def downx_step(step, ways="lh"):
        @pl.loop(0, DK)
        def _(k):
            sign = 1 - 2 * k
            if "l" in ways:
                ring(step, k, k, sign, s0dx.at[0], rldx, dlx_ss, dlx_rs, 4, downx_dot(k))
            if "h" in ways and step < 3:
                ring(step, k, k, -sign, s0dx.at[1], rsdx, dhx_ss, dhx_rs, 3, downx_dot(k))

    def down_end():
        @pl.loop(0, DK)
        def _(k):
            sign = 1 - 2 * k
            find[...] = ring_end(k, k, sign, rld, rsd, dl_ss, dl_rs, dh_ss, dh_rs, down_dot(k))
            xsd[k] = find[other_u, :].astype(BF)
            dx_copy(k).start()
            accd[k] = find[own_u, :]

        @pl.loop(0, DK)
        def _(k):
            sign = 1 - 2 * k
            accd[k + DK] = ring_end(
                k, k, sign, rldx, rsdx, dlx_ss, dlx_rs, dhx_ss, dhx_rs, downx_dot(k))

    def da_out(i):
        return lc(dab.at[i], (nd, ndm, ndv)[i], da_sem.at[i])

    def down_update():
        lc(wd.at[rows_of(d, 224), :], dab.at[0], da_sem.at[0]).wait()
        lc(dm, dab.at[1], da_sem.at[1]).wait()
        lc(dv, dab.at[2], da_sem.at[2]).wait()

        @pl.loop(0, DK)
        def _(k):
            dx_copy(k).wait()
            accd[k] += xrd[k].astype(F32)

        @pl.loop(0, 2 * DK)
        def _(k):
            cols = rows_of(k, DC)

            @pl.loop(0, 7)
            def _(i):
                sub = rows_of(i, 32)
                new = adamw(
                    dab[0, sub, cols], dab[1, sub, cols], dab[2, sub, cols], accd[k, sub, :])
                for n in range(3):
                    dab[n, sub, cols] = new[n]

        for i in range(3):
            da_out(i).start()

    def gate_dot(j):
        def dot(dest):
            return dot_nn(xt_all[rows_of(dest, ZR), :], gu[2 * j])
        return dot

    own_w = rows_of(xl, 64)
    other_w = rows_of(1 - xl, 64)

    def up_half(j, dest, side):
        rows = pl.ds(pl.multiple_of(dest * ZR + side * 64, 64), 64)
        return dot_nn(xt_all[rows, :], gu[2 * j + 1])

    def xp_copy(j, dest):
        par = lax.rem(j, 2)
        return rc(xps.at[par, dest], xpr.at[j, dest], xp_ss.at[par, dest], xp_rs.at[j, dest], xdev)

    def up_pre(j):
        par = lax.rem(j, 2)
        sign = 2 * par - 1

        @pl.loop(0, NZ)
        def _(i):
            away = sign * (1 - 2 * lax.rem(i, 2)) * (4 - lax.div(i + 1, 2))
            dest = zmod(z + away)

            @pl.when(j >= 2)
            def _():
                xp_copy(j, dest).wait_send()

            xps[par, dest] = up_half(j, dest, 1 - xl).astype(BF)
            xp_copy(j, dest).start()

    def up_dot(j):
        def dot(dest):
            val = up_half(j, dest, xl)
            xp_copy(j, dest).wait_recv()
            return val + xpr[j, dest].astype(F32)
        return dot

    def x_copy(j):
        par = lax.rem(j, 2)
        return rc(xs.at[par], xr.at[j], x_ss.at[par], x_rs.at[j], xdev)

    def ab_in(t, j):
        @pl.when(j >= 1)
        def _():
            ob_wait(t)

        cols = rows_of(j, CB)
        w, m, v = ((wg, gm, gv), (wu, um, uv))[t]
        lc(w.at[rows_of(d, 64), cols], abuf.at[t, 0], ab_sem.at[t, 0]).start()
        lc(m.at[:, cols], abuf.at[t, 1], ab_sem.at[t, 1]).start()
        lc(v.at[:, cols], abuf.at[t, 2], ab_sem.at[t, 2]).start()

    def ob_wait(t):
        for n in range(3):
            lc(abuf.at[t, n], ng.at[:, pl.ds(0, CB)], ob_sem.at[t, n]).wait()

    def gate_step(step, j):
        par = lax.rem(j, 2)
        sign = 1 - 2 * par
        ring(step, j, par, sign, s0.at[0], rl, l_ss, l_rs, 4, gate_dot(j))
        if step < 3:
            ring(step, j, par, -sign, s0.at[1], rs, h_ss, h_rs, 3, gate_dot(j))

    def up_step(step, j):
        par = lax.rem(j, 2)
        sign = 2 * par - 1
        ring(step, j, par, sign, s0x.at[0], rlx, lx_ss, lx_rs, 4, up_dot(j))
        if step < 3:
            ring(step, j, par, -sign, s0x.at[1], rsx, hx_ss, hx_rs, 3, up_dot(j))

    def gate_end(j):
        par = lax.rem(j, 2)
        fin[...] = ring_end(j, par, 1 - 2 * par, rl, rs, l_ss, l_rs, h_ss, h_rs, gate_dot(j))
        xs[par] = fin[other_w, :].astype(BF)
        x_copy(j).start()
        acc[par] = fin[own_w, :]

    def up_end(j):
        par = lax.rem(j, 2)
        acc[2] = ring_end(j, par, 2 * par - 1, rlx, rsx, lx_ss, lx_rs, hx_ss, hx_rs, up_dot(j))
        update(1, j, 2)

    def gate_update(j):
        x_copy(j).wait()
        par = lax.rem(j, 2)
        acc[par] += xr[j].astype(F32)
        update(0, j, par)

    def update(t, j, slot):
        for n in range(3):
            lc(gm.at[:, pl.ds(0, CB)], abuf.at[t, n], ab_sem.at[t, n]).wait()

        @pl.loop(0, 4)
        def _(i):
            sub = rows_of(i, 16)
            new = adamw(abuf[t, 0, sub, :], abuf[t, 1, sub, :], abuf[t, 2, sub, :], acc[slot, sub, :])
            for n in range(3):
                abuf[t, n, sub, :] = new[n]

        cols = rows_of(j, CB)
        refs = ((ng, ngm, ngv), (nu, num, nuv))[t]
        for n in range(3):
            lc(abuf.at[t, n], refs[n].at[:, cols], ob_sem.at[t, n]).start()

    def ig_add(q):
        par = lax.rem(q, 2)
        lc(wg.at[:, pl.ds(0, CB)], wgb.at[par], wg_sem.at[par]).wait()

        @pl.loop(0, 4)
        def _(i):
            sub = rows_of(i, 128)
            val = dot_nt(gu[q, sub, :], wgb[par])

            @pl.when(q == 0)
            def _():
                igacc[sub, :] = val

            @pl.when(q > 0)
            def _():
                igacc[sub, :] += val

        @pl.when(q + 2 < NQ)
        def _():
            wg_start(q + 2, par)

    def ig_copy(k):
        return rc(igs.at[k - 1], igr.at[k - 1], ig_ss.at[k - 1], ig_rs.at[k - 1], cdev(k))

    def ig_send():
        for k in (2, 1, 3):
            igs[k - 1] = igacc[rows_of(lax.rem(c + k, 4), 128), :].astype(BF)
            ig_copy(k).start()

    def ig_end():
        for k in (2, 1, 3):
            ig_copy(k).wait()
        val = igacc[own_c, :]
        for k in range(3):
            val += igr[k].astype(F32)
        igo[...] = val.astype(BF)
        lc(igo, ig_out, igo_sem).start()

    def relayed(copy):
        copy(0).wait_recv()
        copy(2).start()
        copy(0).wait_send()
        copy(1).wait()
        copy(2).wait()

    ht_pass(0, 3)
    relayed(do_copy)
    ht_send(3, 5)
    ht_wait(0, 1)
    down_step(0, "l")
    downx_pre(0, "l")
    ht_wait(1, 3)
    down_step(0, "h")
    downx_pre(0, "h")

    ht_pass(3, 5)
    ht_send(5, 7)
    ht_wait(3, 5)
    down_step(1)
    downx_pre(1)
    ht_pass(5, 7)
    ht_send(7, 8)
    stage_a(0)
    downx_step(0)

    ht_wait(5, 7)
    down_step(2)
    downx_pre(2)
    for n in range(2):
        xt_copy(n).start()
    ht_pass(7, 8)
    stage_a(1)
    downx_step(1)
    stage_b(0)

    ht_wait(7, 8)
    down_step(3)
    downx_pre(3)
    downx_pre(4)
    stage_a(2)
    downx_step(2)
    pass_b(0)
    stage_b(1)
    relayed(xt_copy)

    def up_gate_ready(q):
        for n in (2, 3):
            b_copy(q, n).wait_recv()

    @pl.loop(0, NQ + 4)
    def _(t):
        for step in (3, 2, 1, 0):
            q = t - step
            job = lax.div(q, 2)

            @pl.when((q >= 0) & (q < NQ) & (lax.rem(q, 2) == 0))
            def _():
                if step == 0:
                    up_gate_ready(q)
                gate_step(step, job)

            @pl.when((q >= 0) & (q < NQ) & (lax.rem(q, 2) == 1))
            def _():
                if step == 3:
                    ab_in(1, job)
                up_step(step, job)

        @pl.when((t < NQ) & (lax.rem(t, 2) == 0))
        def _():
            up_gate_ready(t + 1)
            up_pre(lax.div(t, 2))

        half = lax.div(t, 2)

        @pl.when((lax.rem(t, 2) == 0) & (half + 1 < NB))
        def _():
            pass_b(half + 1)

        @pl.when((lax.rem(t, 2) == 0) & (half + 3 < NB))
        def _():
            stage_a(half + 3)

        @pl.when((lax.rem(t, 2) == 1) & (half + 2 < NB))
        def _():
            stage_b(half + 2)

        @pl.when((t >= 4) & (lax.rem(t, 2) == 0))
        def _():
            gate_end(lax.div(t - 4, 2))

        @pl.when((t >= 5) & (lax.rem(t, 2) == 1))
        def _():
            up_end(lax.div(t - 5, 2))

        @pl.when((t >= 7) & (lax.rem(t, 2) == 1))
        def _():
            gate_update(lax.div(t - 7, 2))

        @pl.when((t >= 5) & (lax.rem(t, 2) == 1))
        def _():
            ab_in(0, lax.div(t - 5, 2))

        @pl.when(t < NQ)
        def _():
            ig_add(t)

        @pl.when(t == 0)
        def _():
            downx_step(3)

        @pl.when(t == 2)
        def _():
            down_end()

        @pl.when(t == 3)
        def _():
            down_update()

        @pl.when(t == NQ)
        def _():
            ig_send()

    gate_update(NB - 1)
    ig_end()
    for i in range(3):
        da_out(i).wait()
    lc(igo, ig_out, igo_sem).wait()
    for par in range(2):
        ob_wait(par)
        for k in (2, 1, 3):
            a_copy(0, par, k).wait_send()

    @pl.loop(0, NZ)
    def _(i):
        for n in range(4):
            ht_copy(i, n).wait_send()

    @pl.loop(0, NQ)
    def _(q):
        for n in range(4):
            b_copy(q, n).wait_send()

    @pl.loop(0, NZ)
    def _(i):
        for j in (NB - 2, NB - 1):
            xp_copy(j, i).wait_send()


def hand_over(*refs):
    src, dst, buf = refs[:10], refs[10:20], refs[20:30]
    ins = [pltpu.make_async_copy(src[i], buf[i], refs[30].at[i]) for i in range(10)]
    outs = [pltpu.make_async_copy(buf[i], dst[i], refs[31].at[i]) for i in range(10)]
    for copy in ins:
        copy.start()
    for i in range(10):
        ins[i].wait()
        outs[i].start()
    for copy in outs:
        copy.wait()


def on_device(*args):
    vm = pltpu.VMEM
    dma = pltpu.SemaphoreType.DMA
    scratch = [
        vm((512, 1024), BF),
        vm((1024, 512), BF),
        vm((3584, 512), BF),
        vm((NQ, 512, CB), BF),
        vm((2, CB, 1024), BF),
        vm((2, 1024, CB), BF),
        vm((2, 3, 128, CB), BF),
        vm((2, 128, CB), F32),
        vm((NB, 3, 128, CB), BF),
        vm((2, 2, ZR, CB), BF),
        vm((NB, 4, ZR, CB), BF),
        vm((NB, 3, ZR, CB), BF),
        vm((ZR, CB), F32),
        vm((3, 64, CB), F32),
        vm((2, 64, CB), BF),
        vm((NB, 64, CB), BF),
        vm((2, 3, 64, CB), BF),
        vm((2, 2, 64, CB), BF),
        vm((NB, 4, 64, CB), BF),
        vm((NB, 3, 64, CB), BF),
        vm((2, NZ, 64, CB), BF),
        vm((NB, NZ, 64, CB), BF),
        vm((2, DK, UR, DC), BF),
        vm((DK, 4, UR, DC), BF),
        vm((DK, 3, UR, DC), BF),
        vm((UR, DC), F32),
        vm((2 * DK, 224, DC), F32),
        vm((DK, 224, DC), BF),
        vm((DK, 224, DC), BF),
        vm((3, 224, 1024), BF),
        vm((2, DK, 224, DC), BF),
        vm((DK, 4, 224, DC), BF),
        vm((DK, 3, 224, DC), BF),
        vm((DK, NZ, 224, DC), BF),
        vm((DK, NZ, 224, DC), BF),
        vm((512, 1024), F32),
        vm((3, 128, 1024), BF),
        vm((3, 128, 1024), BF),
        vm((128, 1024), BF),
        dma((3,)), dma((3,)), dma((3,)), dma((3,)),
        dma((NZ, 4)), dma((NZ, 4)),
        dma((2, 3)), dma((NB, 3)),
        dma((NQ, 4)), dma((NQ, 4)),
        dma((2, 4)), dma((NB, 4)), dma((2, 3)), dma((NB, 3)),
        dma((2,)), dma((NB,)),
        dma((2, 4)), dma((NB, 4)), dma((2, 3)), dma((NB, 3)),
        dma((2, NZ)), dma((NB, NZ)),
        dma((DK, 4)), dma((DK, 4)), dma((DK, 3)), dma((DK, 3)),
        dma((DK,)), dma((DK,)),
        dma((DK, 4)), dma((DK, 4)), dma((DK, 3)), dma((DK, 3)),
        dma((DK, NZ)), dma((DK, NZ)),
        dma((3,)), dma((3,)),
        dma((2,)), dma((2,)), dma((2, 3)), dma((2, 3)), dma((3,)), dma(()),
    ]
    shapes = [(128, 1024)] + [(64, 3584)] * 6 + [(224, 1024)] * 3
    in_vmem = pl.BlockSpec(memory_space=pltpu.VMEM)
    in_any = pl.BlockSpec(memory_space=pl.ANY)
    shapes = [jax.ShapeDtypeStruct(s, BF) for s in shapes]
    results = pl.pallas_call(
        kernel,
        out_shape=shapes,
        in_specs=[in_vmem] * 4 + [in_any] * 9,
        out_specs=[in_any] * 10,
        scratch_shapes=scratch,
        compiler_params=pltpu.CompilerParams(
            collective_id=0, has_side_effects=True, vmem_limit_bytes=60 * 2**20
        ),
        cost_estimate=pl.CostEstimate(
            flops=22548578304, bytes_accessed=34000000, transcendentals=4000000
        ),
    )(*args)
    return pl.pallas_call(
        hand_over,
        out_shape=shapes,
        in_specs=[in_any] * 10,
        out_specs=[in_any] * 10,
        scratch_shapes=[vm(s.shape, BF) for s in shapes] + [dma((10,)), dma((10,))],
    )(*results)


def solution(mesh):
    act = P(("depth", "col"), "row")
    pre = P(("depth", "row"), "col")
    wide = P("row", "col")
    tall = P("col", "row")
    wide_own = P(("row", "depth"), "col")
    tall_own = P(("col", "depth"), "row")
    return jax.shard_map(
        on_device,
        mesh=mesh,
        in_specs=(act, act, pre, pre, wide, wide, tall) + (wide_own,) * 4 + (tall_own,) * 2,
        out_specs=(act,) + (wide_own,) * 6 + (tall_own,) * 3,
        check_vma=False,
    )
```

```python
import jax
import jax.numpy as jnp
from jax import lax
from jax.experimental import pallas as pl
from jax.experimental.pallas import tpu as pltpu
from jax.sharding import PartitionSpec as P

BF = jnp.bfloat16
F32 = jnp.float32
MESH = pl.DeviceIdType.MESH

lr_rate = 0.0003
beta_one = 0.9
beta_two = 0.95
decay_rate = 0.1
eps_value = 1e-08
correct_one = 1.0 - 0.9**20
correct_two = 1.0 - 0.95**20

NZ = 8
CB = 512
NB = 7
NQ = 2 * NB
ZR = 128
UR = 448
DK = 2
DC = 256


def adamw(weight, first, second, grad):
    first_new = beta_one * first.astype(F32) + (1.0 - beta_one) * grad
    second_new = beta_two * second.astype(F32) + (1.0 - beta_two) * grad * grad
    wval = weight.astype(F32)
    step_val = (
        first_new / correct_one / (jnp.sqrt(second_new / correct_two) + eps_value)
        + decay_rate * wval
    )
    return (
        (wval - lr_rate * step_val).astype(BF),
        first_new.astype(BF),
        second_new.astype(BF),
    )


def dot_nn(a, b):
    return lax.dot_general(a, b, (((1,), (0,)), ((), ())), preferred_element_type=F32)


def dot_nt(a, b):
    return lax.dot_general(a, b, (((1,), (1,)), ((), ())), preferred_element_type=F32)


def rows_of(index, size):
    return pl.ds(pl.multiple_of(index * size, size), size)


def kernel(
    x_ref, do_ref, gp_ref, up_ref, wg, wu, wd, gm, gv, um, uv, dm, dv,
    ig_out, ng, ngm, ngv, nu, num, nuv, nd, ndm, ndv,
    do_all, xt_all, ht_all, gu, wdb, wgb, a_s, a_own, a_r,
    s0, rl, rs, fin, acc, xs, xr, abuf, s0x, rlx, rsx, xps, xpr,
    s0d, rld, rsd, find, accd, xsd, xrd, dab, s0dx, rldx, rsdx, xpsd, xprd,
    igacc, igs, igr, igo,
    do_ss, do_rs, xt_ss, xt_rs, ht_ss, ht_rs, a_ss, a_rs, b_ss, b_rs,
    l_ss, l_rs, h_ss, h_rs, x_ss, x_rs,
    lx_ss, lx_rs, hx_ss, hx_rs, xp_ss, xp_rs,
    dl_ss, dl_rs, dh_ss, dh_rs, dx_ss, dx_rs,
    dlx_ss, dlx_rs, dhx_ss, dhx_rs, dxp_ss, dxp_rs,
    ig_ss, ig_rs, wd_sem, wg_sem, ab_sem, ob_sem, da_sem, igo_sem,
):
    d = lax.axis_index("depth")
    r = lax.axis_index("row")
    c = lax.axis_index("col")
    z = lax.div(d, 2)
    xl = lax.rem(d, 2)

    def zmod(v):
        return lax.rem(v + 16, NZ)

    def zdev(v):
        return (2 * zmod(v) + xl, r, c)

    xdev = (2 * z + 1 - xl, r, c)

    def ydev(k):
        return (d, lax.rem(r + k, 4), c)

    def cdev(k):
        return (d, r, lax.rem(c + k, 4))

    def rc(src, dst, ss, rsem, dev):
        return pltpu.make_async_remote_copy(
            src_ref=src, dst_ref=dst, send_sem=ss, recv_sem=rsem,
            device_id=dev, device_id_type=MESH,
        )

    def lc(src, dst, sem):
        return pltpu.make_async_copy(src, dst, sem)

    def wd_copy(j, par):
        return lc(wd.at[rows_of(j, CB), :], wdb.at[par], wd_sem.at[par])

    def wg_start(q, par):
        cols = rows_of(lax.div(q, 2), CB)

        @pl.when(par == 0)
        def _():
            lc(wg.at[:, cols], wgb.at[0], wg_sem.at[0]).start()

        @pl.when(par == 1)
        def _():
            lc(wu.at[:, cols], wgb.at[1], wg_sem.at[1]).start()

    for p in range(2):
        wd_copy(p, p).start()
    lc(wg.at[:, pl.ds(0, CB)], wgb.at[0], wg_sem.at[0]).start()
    lc(wu.at[:, pl.ds(0, CB)], wgb.at[1], wg_sem.at[1]).start()
    lc(wd.at[rows_of(d, 224), :], dab.at[0], da_sem.at[0]).start()
    lc(dm, dab.at[1], da_sem.at[1]).start()
    lc(dv, dab.at[2], da_sem.at[2]).start()

    barrier = pltpu.get_barrier_semaphore()
    partners = [zdev(z + 1), zdev(z - 1), xdev]
    partners += [ydev(k) for k in (1, 2, 3)] + [cdev(k) for k in (1, 2, 3)]
    for dev in partners:
        pl.semaphore_signal(barrier, inc=1, device_id=dev, device_id_type=MESH)

    own_c = rows_of(c, 128)
    own_r = rows_of(r, 128)

    @pl.loop(0, NB)
    def _(j):
        cols = rows_of(j, CB)
        g = gp_ref[:, cols].astype(F32)
        h = g * jax.nn.sigmoid(g) * up_ref[:, cols].astype(F32)
        ht_all[cols, own_r] = h.T.astype(BF)

    pl.semaphore_wait(barrier, len(partners))

    c_far = lax.rem(c + 2, 4)
    c_near = c + 1 - 2 * lax.rem(c, 2)
    far_dev, near_dev = (d, r, c_far), (d, r, c_near)

    def do_copy(n):
        rows = own_c if n < 2 else rows_of(c_far, 128)
        view = do_all.at[rows, :]
        return rc(do_ref if n < 2 else view, view, do_ss.at[n], do_rs.at[n],
                  near_dev if n else far_dev)

    for n in range(2):
        do_copy(n).start()
    do_all[own_c, :] = do_ref[...]

    def row_dev(n):
        return ydev(3 if n % 2 else 1)

    def row_block(n):
        return rows_of(r if n < 2 else lax.rem(r + (1 if n % 2 else 3), 4), 128)

    def ht_copy(i, n):
        away = (2 * lax.rem(i, 2) - 1) * (4 - lax.div(i + 1, 2))
        first = zmod(z + away) * UR
        if n < 2:
            rows = pl.ds(pl.multiple_of(first, 64), UR)
        else:
            rows = pl.ds(pl.multiple_of(first + (n - 2) * 224, 32), 224)
        view = ht_all.at[rows, row_block(n)]
        return rc(view, view, ht_ss.at[i, n], ht_rs.at[i, n], row_dev(n))

    def ht_send(first, last):
        @pl.loop(first, last)
        def _(i):
            for n in range(2):
                ht_copy(i, n).start()

    def ht_pass(first, last):
        @pl.loop(first, last)
        def _(i):
            for n in range(2):
                ht_copy(i, n).wait_recv()
                ht_copy(i, n + 2).start()

    def ht_wait(first, last):
        @pl.loop(first, last)
        def _(i):
            for n in (2, 3):
                ht_copy(i, n).wait_recv()

    ht_send(0, 3)

    xt_all[:, own_c] = x_ref[...].T

    def xt_copy(n):
        view = xt_all.at[:, own_c if n < 2 else rows_of(c_far, 128)]
        return rc(view, view, xt_ss.at[n], xt_rs.at[n], near_dev if n else far_dev)

    def a_copy(j, par, k):
        return rc(a_s.at[par, k - 1], a_r.at[j, k - 1], a_ss.at[par, k - 1],
                  a_rs.at[j, k - 1], ydev(k))

    def stage_a(j):
        par = lax.rem(j, 2)
        wd_copy(j, par).wait()

        @pl.when(j >= 2)
        def _():
            for k in (2, 1, 3):
                a_copy(j, par, k).wait_send()

        def part(k):
            return dot_nt(do_all[rows_of(lax.rem(r + k, 4), 128), :], wdb[par])

        for k in (2, 1, 3):
            a_s[par, k - 1] = part(k).astype(BF)
            a_copy(j, par, k).start()
        a_own[par] = part(0)

        @pl.when(j + 2 < NB)
        def _():
            wd_copy(j + 2, par).start()

    def b_copy(q, n):
        if n < 2:
            view = gu.at[q, row_block(n), :]
        else:
            first = lax.rem(r + (1 if n % 2 else 3), 4) * 128 + (n - 2) * 64
            view = gu.at[q, pl.ds(pl.multiple_of(first, 64), 64), :]
        return rc(view, view, b_ss.at[q, n], b_rs.at[q, n], row_dev(n))

    def pass_b(j):
        for t in range(2):
            for n in range(2):
                b_copy(2 * j + t, n).wait_recv()
                b_copy(2 * j + t, n + 2).start()

    def stage_b(j):
        par = lax.rem(j, 2)
        for k in (2, 1, 3):
            a_copy(j, par, k).wait_recv()

        @pl.loop(0, 8)
        def _(i):
            sub = rows_of(i, 16)
            cols = rows_of(j, CB)
            hg = a_own[par, sub, :]
            for k in range(3):
                hg += a_r[j, k, sub, :].astype(F32)
            g = gp_ref[sub, cols].astype(F32)
            u = up_ref[sub, cols].astype(F32)
            sig = jax.nn.sigmoid(g)
            dst = pl.ds(pl.multiple_of(r * 128 + i * 16, 16), 16)
            gu[2 * j, dst, :] = (hg * u * sig * (1.0 + g * (1.0 - sig))).astype(BF)
            gu[2 * j + 1, dst, :] = (hg * (g * sig)).astype(BF)

        for t in range(2):
            for n in range(2):
                b_copy(2 * j + t, n).start()

    def ring(step, job, par, sign, first, slots, ssem, rsem, hops, dot):
        dest = zmod(z + sign * (hops - step))
        val = dot(dest)
        if step == 0:
            src = first.at[par]
        else:
            src = slots.at[job, step - 1]
            prev = first.at[par] if step == 1 else slots.at[job, step - 2]
            rc(prev, src, ssem.at[par, step - 1], rsem.at[job, step - 1], zdev(z + sign)).wait()
            val += src[...].astype(F32)
        src[...] = val.astype(BF)
        rc(src, slots.at[job, step], ssem.at[par, step], rsem.at[job, step],
           zdev(z + sign)).start()

    def ring_end(job, par, sign, slots_l, slots_h, lss, lrs, hss, hrs, dot):
        val = dot(z)
        last = slots_l.at[job, 3]
        rc(slots_l.at[job, 2], last, lss.at[par, 3], lrs.at[job, 3], zdev(z + sign)).wait()
        val += last[...].astype(F32)
        last = slots_h.at[job, 2]
        rc(slots_h.at[job, 1], last, hss.at[par, 2], hrs.at[job, 2], zdev(z - sign)).wait()
        return val + last[...].astype(F32)

    def down_dot(k):
        def dot(dest):
            return dot_nn(ht_all[rows_of(dest, UR), :], do_all[:, rows_of(k, DC)])
        return dot

    own_u = rows_of(xl, 224)
    other_u = rows_of(1 - xl, 224)

    def half_dot(k, dest, side):
        rows = pl.ds(pl.multiple_of(dest * UR + side * 224, 32), 224)
        return dot_nn(ht_all[rows, :], do_all[:, rows_of(k + DK, DC)])

    def dxp_copy(k, dest):
        return rc(xpsd.at[k, dest], xprd.at[k, dest], dxp_ss.at[k, dest], dxp_rs.at[k, dest], xdev)

    def downx_pre(step, ways="lh"):
        @pl.loop(0, DK)
        def _(k):
            sign = 1 - 2 * k
            dests = []
            if "l" in ways:
                dests.append(zmod(z + sign * (4 - step)))
            if "h" in ways and step < 3:
                dests.append(zmod(z - sign * (3 - step)))
            for dest in dests:
                xpsd[k, dest] = half_dot(k, dest, 1 - xl).astype(BF)
                dxp_copy(k, dest).start()

    def downx_dot(k):
        def dot(dest):
            val = half_dot(k, dest, xl)
            dxp_copy(k, dest).wait()
            return val + xprd[k, dest].astype(F32)
        return dot

    def dx_copy(k):
        return rc(xsd.at[k], xrd.at[k], dx_ss.at[k], dx_rs.at[k], xdev)

    def down_step(step, ways="lh"):
        @pl.loop(0, DK)
        def _(k):
            sign = 1 - 2 * k
            if "l" in ways:
                ring(step, k, k, sign, s0d.at[0], rld, dl_ss, dl_rs, 4, down_dot(k))
            if "h" in ways and step < 3:
                ring(step, k, k, -sign, s0d.at[1], rsd, dh_ss, dh_rs, 3, down_dot(k))

    def downx_step(step, ways="lh"):
        @pl.loop(0, DK)
        def _(k):
            sign = 1 - 2 * k
            if "l" in ways:
                ring(step, k, k, sign, s0dx.at[0], rldx, dlx_ss, dlx_rs, 4, downx_dot(k))
            if "h" in ways and step < 3:
                ring(step, k, k, -sign, s0dx.at[1], rsdx, dhx_ss, dhx_rs, 3, downx_dot(k))

    def down_end():
        @pl.loop(0, DK)
        def _(k):
            sign = 1 - 2 * k
            find[...] = ring_end(k, k, sign, rld, rsd, dl_ss, dl_rs, dh_ss, dh_rs, down_dot(k))
            xsd[k] = find[other_u, :].astype(BF)
            dx_copy(k).start()
            accd[k] = find[own_u, :]

        @pl.loop(0, DK)
        def _(k):
            sign = 1 - 2 * k
            accd[k + DK] = ring_end(
                k, k, sign, rldx, rsdx, dlx_ss, dlx_rs, dhx_ss, dhx_rs, downx_dot(k))

    def da_out(i):
        return lc(dab.at[i], (nd, ndm, ndv)[i], da_sem.at[i])

    def down_update():
        lc(wd.at[rows_of(d, 224), :], dab.at[0], da_sem.at[0]).wait()
        lc(dm, dab.at[1], da_sem.at[1]).wait()
        lc(dv, dab.at[2], da_sem.at[2]).wait()

        @pl.loop(0, DK)
        def _(k):
            dx_copy(k).wait()
            accd[k] += xrd[k].astype(F32)

        @pl.loop(0, 2 * DK)
        def _(k):
            cols = rows_of(k, DC)

            @pl.loop(0, 7)
            def _(i):
                sub = rows_of(i, 32)
                new = adamw(
                    dab[0, sub, cols], dab[1, sub, cols], dab[2, sub, cols], accd[k, sub, :])
                for n in range(3):
                    dab[n, sub, cols] = new[n]

        for i in range(3):
            da_out(i).start()

    def gate_dot(j):
        def dot(dest):
            return dot_nn(xt_all[rows_of(dest, ZR), :], gu[2 * j])
        return dot

    own_w = rows_of(xl, 64)
    other_w = rows_of(1 - xl, 64)

    def up_half(j, dest, side):
        rows = pl.ds(pl.multiple_of(dest * ZR + side * 64, 64), 64)
        return dot_nn(xt_all[rows, :], gu[2 * j + 1])

    def xp_copy(j, dest):
        par = lax.rem(j, 2)
        return rc(xps.at[par, dest], xpr.at[j, dest], xp_ss.at[par, dest], xp_rs.at[j, dest], xdev)

    def up_pre(j):
        par = lax.rem(j, 2)
        sign = 2 * par - 1

        @pl.loop(0, NZ)
        def _(i):
            away = sign * (1 - 2 * lax.rem(i, 2)) * (4 - lax.div(i + 1, 2))
            dest = zmod(z + away)

            @pl.when(j >= 2)
            def _():
                xp_copy(j, dest).wait_send()

            xps[par, dest] = up_half(j, dest, 1 - xl).astype(BF)
            xp_copy(j, dest).start()

    def up_dot(j):
        def dot(dest):
            val = up_half(j, dest, xl)
            xp_copy(j, dest).wait_recv()
            return val + xpr[j, dest].astype(F32)
        return dot

    def x_copy(j):
        par = lax.rem(j, 2)
        return rc(xs.at[par], xr.at[j], x_ss.at[par], x_rs.at[j], xdev)

    def ab_in(t, j):
        @pl.when(j >= 1)
        def _():
            ob_wait(t)

        cols = rows_of(j, CB)
        w, m, v = ((wg, gm, gv), (wu, um, uv))[t]
        lc(w.at[rows_of(d, 64), cols], abuf.at[t, 0], ab_sem.at[t, 0]).start()
        lc(m.at[:, cols], abuf.at[t, 1], ab_sem.at[t, 1]).start()
        lc(v.at[:, cols], abuf.at[t, 2], ab_sem.at[t, 2]).start()

    def ob_wait(t):
        for n in range(3):
            lc(abuf.at[t, n], ng.at[:, pl.ds(0, CB)], ob_sem.at[t, n]).wait()

    def gate_step(step, j):
        par = lax.rem(j, 2)
        sign = 1 - 2 * par
        ring(step, j, par, sign, s0.at[0], rl, l_ss, l_rs, 4, gate_dot(j))
        if step < 3:
            ring(step, j, par, -sign, s0.at[1], rs, h_ss, h_rs, 3, gate_dot(j))

    def up_step(step, j):
        par = lax.rem(j, 2)
        sign = 2 * par - 1
        ring(step, j, par, sign, s0x.at[0], rlx, lx_ss, lx_rs, 4, up_dot(j))
        if step < 3:
            ring(step, j, par, -sign, s0x.at[1], rsx, hx_ss, hx_rs, 3, up_dot(j))

    def gate_end(j):
        par = lax.rem(j, 2)
        fin[...] = ring_end(j, par, 1 - 2 * par, rl, rs, l_ss, l_rs, h_ss, h_rs, gate_dot(j))
        xs[par] = fin[other_w, :].astype(BF)
        x_copy(j).start()
        acc[par] = fin[own_w, :]

    def up_end(j):
        par = lax.rem(j, 2)
        acc[2] = ring_end(j, par, 2 * par - 1, rlx, rsx, lx_ss, lx_rs, hx_ss, hx_rs, up_dot(j))
        update(1, j, 2)

    def gate_update(j):
        x_copy(j).wait()
        par = lax.rem(j, 2)
        acc[par] += xr[j].astype(F32)
        update(0, j, par)

    def update(t, j, slot):
        for n in range(3):
            lc(gm.at[:, pl.ds(0, CB)], abuf.at[t, n], ab_sem.at[t, n]).wait()

        @pl.loop(0, 4)
        def _(i):
            sub = rows_of(i, 16)
            new = adamw(abuf[t, 0, sub, :], abuf[t, 1, sub, :], abuf[t, 2, sub, :], acc[slot, sub, :])
            for n in range(3):
                abuf[t, n, sub, :] = new[n]

        cols = rows_of(j, CB)
        refs = ((ng, ngm, ngv), (nu, num, nuv))[t]
        for n in range(3):
            lc(abuf.at[t, n], refs[n].at[:, cols], ob_sem.at[t, n]).start()

    def ig_add(q):
        par = lax.rem(q, 2)
        lc(wg.at[:, pl.ds(0, CB)], wgb.at[par], wg_sem.at[par]).wait()

        @pl.loop(0, 4)
        def _(i):
            sub = rows_of(i, 128)
            val = dot_nt(gu[q, sub, :], wgb[par])

            @pl.when(q == 0)
            def _():
                igacc[sub, :] = val

            @pl.when(q > 0)
            def _():
                igacc[sub, :] += val

        @pl.when(q + 2 < NQ)
        def _():
            wg_start(q + 2, par)

    def ig_copy(k):
        return rc(igs.at[k - 1], igr.at[k - 1], ig_ss.at[k - 1], ig_rs.at[k - 1], cdev(k))

    def ig_send():
        for k in (2, 1, 3):
            igs[k - 1] = igacc[rows_of(lax.rem(c + k, 4), 128), :].astype(BF)
            ig_copy(k).start()

    def ig_end():
        for k in (2, 1, 3):
            ig_copy(k).wait()
        val = igacc[own_c, :]
        for k in range(3):
            val += igr[k].astype(F32)
        igo[...] = val.astype(BF)
        lc(igo, ig_out, igo_sem).start()

    def relayed(copy):
        copy(0).wait_recv()
        copy(2).start()
        copy(0).wait_send()
        copy(1).wait()
        copy(2).wait()

    ht_pass(0, 3)
    relayed(do_copy)
    ht_send(3, 5)
    ht_wait(0, 1)
    down_step(0, "l")
    downx_pre(0, "l")
    ht_wait(1, 3)
    down_step(0, "h")
    downx_pre(0, "h")

    ht_pass(3, 5)
    ht_send(5, 7)
    ht_wait(3, 5)
    down_step(1)
    downx_pre(1)
    ht_pass(5, 7)
    ht_send(7, 8)
    stage_a(0)
    downx_step(0)

    ht_wait(5, 7)
    down_step(2)
    downx_pre(2)
    for n in range(2):
        xt_copy(n).start()
    ht_pass(7, 8)
    stage_a(1)
    downx_step(1)
    stage_b(0)

    ht_wait(7, 8)
    down_step(3)
    downx_pre(3)
    downx_pre(4)
    stage_a(2)
    downx_step(2)
    pass_b(0)
    stage_b(1)
    relayed(xt_copy)

    def up_gate_ready(q):
        for n in (2, 3):
            b_copy(q, n).wait_recv()

    @pl.loop(0, NQ + 4)
    def _(t):
        for step in (3, 2, 1, 0):
            q = t - step
            job = lax.div(q, 2)

            @pl.when((q >= 0) & (q < NQ) & (lax.rem(q, 2) == 0))
            def _():
                if step == 0:
                    up_gate_ready(q)
                gate_step(step, job)

            @pl.when((q >= 0) & (q < NQ) & (lax.rem(q, 2) == 1))
            def _():
                if step == 3:
                    ab_in(1, job)
                up_step(step, job)

        @pl.when((t < NQ) & (lax.rem(t, 2) == 0))
        def _():
            up_gate_ready(t + 1)
            up_pre(lax.div(t, 2))

        half = lax.div(t, 2)

        @pl.when((lax.rem(t, 2) == 0) & (half + 3 < NB))
        def _():
            stage_a(half + 3)

        @pl.when((lax.rem(t, 2) == 1) & (half + 2 < NB))
        def _():
            stage_b(half + 2)

        @pl.when((t >= 4) & (lax.rem(t, 2) == 0))
        def _():
            gate_end(lax.div(t - 4, 2))

        @pl.when((t >= 5) & (lax.rem(t, 2) == 1))
        def _():
            up_end(lax.div(t - 5, 2))

        @pl.when((t >= 7) & (lax.rem(t, 2) == 1))
        def _():
            gate_update(lax.div(t - 7, 2))

        @pl.when((t >= 5) & (lax.rem(t, 2) == 1))
        def _():
            ab_in(0, lax.div(t - 5, 2))

        @pl.when(t < NQ)
        def _():
            ig_add(t)

        @pl.when(t == 0)
        def _():
            downx_step(3)

        @pl.when((lax.rem(t, 2) == 0) & (half + 1 < NB))
        def _():
            pass_b(half + 1)

        @pl.when(t == 2)
        def _():
            down_end()

        @pl.when(t == 3)
        def _():
            down_update()

        @pl.when(t == NQ)
        def _():
            ig_send()

    gate_update(NB - 1)
    ig_end()
    for i in range(3):
        da_out(i).wait()
    lc(igo, ig_out, igo_sem).wait()
    for par in range(2):
        ob_wait(par)
        for k in (2, 1, 3):
            a_copy(0, par, k).wait_send()

    @pl.loop(0, NZ)
    def _(i):
        for n in range(4):
            ht_copy(i, n).wait_send()

    @pl.loop(0, NQ)
    def _(q):
        for n in range(4):
            b_copy(q, n).wait_send()

    @pl.loop(0, NZ)
    def _(i):
        for j in (NB - 2, NB - 1):
            xp_copy(j, i).wait_send()


def hand_over(*refs):
    src, dst, buf = refs[:10], refs[10:20], refs[20:30]
    ins = [pltpu.make_async_copy(src[i], buf[i], refs[30].at[i]) for i in range(10)]
    outs = [pltpu.make_async_copy(buf[i], dst[i], refs[31].at[i]) for i in range(10)]
    for copy in ins:
        copy.start()
    for i in range(10):
        ins[i].wait()
        outs[i].start()
    for copy in outs:
        copy.wait()


def on_device(*args):
    vm = pltpu.VMEM
    dma = pltpu.SemaphoreType.DMA
    scratch = [
        vm((512, 1024), BF),
        vm((1024, 512), BF),
        vm((3584, 512), BF),
        vm((NQ, 512, CB), BF),
        vm((2, CB, 1024), BF),
        vm((2, 1024, CB), BF),
        vm((2, 3, 128, CB), BF),
        vm((2, 128, CB), F32),
        vm((NB, 3, 128, CB), BF),
        vm((2, 2, ZR, CB), BF),
        vm((NB, 4, ZR, CB), BF),
        vm((NB, 3, ZR, CB), BF),
        vm((ZR, CB), F32),
        vm((3, 64, CB), F32),
        vm((2, 64, CB), BF),
        vm((NB, 64, CB), BF),
        vm((2, 3, 64, CB), BF),
        vm((2, 2, 64, CB), BF),
        vm((NB, 4, 64, CB), BF),
        vm((NB, 3, 64, CB), BF),
        vm((2, NZ, 64, CB), BF),
        vm((NB, NZ, 64, CB), BF),
        vm((2, DK, UR, DC), BF),
        vm((DK, 4, UR, DC), BF),
        vm((DK, 3, UR, DC), BF),
        vm((UR, DC), F32),
        vm((2 * DK, 224, DC), F32),
        vm((DK, 224, DC), BF),
        vm((DK, 224, DC), BF),
        vm((3, 224, 1024), BF),
        vm((2, DK, 224, DC), BF),
        vm((DK, 4, 224, DC), BF),
        vm((DK, 3, 224, DC), BF),
        vm((DK, NZ, 224, DC), BF),
        vm((DK, NZ, 224, DC), BF),
        vm((512, 1024), F32),
        vm((3, 128, 1024), BF),
        vm((3, 128, 1024), BF),
        vm((128, 1024), BF),
        dma((3,)), dma((3,)), dma((3,)), dma((3,)),
        dma((NZ, 4)), dma((NZ, 4)),
        dma((2, 3)), dma((NB, 3)),
        dma((NQ, 4)), dma((NQ, 4)),
        dma((2, 4)), dma((NB, 4)), dma((2, 3)), dma((NB, 3)),
        dma((2,)), dma((NB,)),
        dma((2, 4)), dma((NB, 4)), dma((2, 3)), dma((NB, 3)),
        dma((2, NZ)), dma((NB, NZ)),
        dma((DK, 4)), dma((DK, 4)), dma((DK, 3)), dma((DK, 3)),
        dma((DK,)), dma((DK,)),
        dma((DK, 4)), dma((DK, 4)), dma((DK, 3)), dma((DK, 3)),
        dma((DK, NZ)), dma((DK, NZ)),
        dma((3,)), dma((3,)),
        dma((2,)), dma((2,)), dma((2, 3)), dma((2, 3)), dma((3,)), dma(()),
    ]
    shapes = [(128, 1024)] + [(64, 3584)] * 6 + [(224, 1024)] * 3
    in_vmem = pl.BlockSpec(memory_space=pltpu.VMEM)
    in_any = pl.BlockSpec(memory_space=pl.ANY)
    shapes = [jax.ShapeDtypeStruct(s, BF) for s in shapes]
    results = pl.pallas_call(
        kernel,
        out_shape=shapes,
        in_specs=[in_vmem] * 4 + [in_any] * 9,
        out_specs=[in_any] * 10,
        scratch_shapes=scratch,
        compiler_params=pltpu.CompilerParams(
            collective_id=0, has_side_effects=True, vmem_limit_bytes=60 * 2**20
        ),
        cost_estimate=pl.CostEstimate(
            flops=22548578304, bytes_accessed=34000000, transcendentals=4000000
        ),
    )(*args)
    return pl.pallas_call(
        hand_over,
        out_shape=shapes,
        in_specs=[in_any] * 10,
        out_specs=[in_any] * 10,
        scratch_shapes=[vm(s.shape, BF) for s in shapes] + [dma((10,)), dma((10,))],
    )(*results)


def solution(mesh):
    act = P(("depth", "col"), "row")
    pre = P(("depth", "row"), "col")
    wide = P("row", "col")
    tall = P("col", "row")
    wide_own = P(("row", "depth"), "col")
    tall_own = P(("col", "depth"), "row")
    return jax.shard_map(
        on_device,
        mesh=mesh,
        in_specs=(act, act, pre, pre, wide, wide, tall) + (wide_own,) * 4 + (tall_own,) * 2,
        out_specs=(act,) + (wide_own,) * 6 + (tall_own,) * 3,
        check_vma=False,
    )
```
